512 devices in a mesh: dom: 128 (over y, z, core), ply: 4 (over x).
Axes of the slice: x: 4, y: 4, z: 16, core: 2. Of those that a mesh axis runs over, the one named last changes fastest.
Arguments:
- state_dofs: float32 [9, 35, 65536], P(None, None, ('dom', 'ply')), may hold values from -6 to 6
- star_matrices: bfloat16 [3, 9, 9, 65536], P(None, None, None, ('dom', 'ply')), may hold values from -0.359375 to 0.359375
- flux_solvers: bfloat16 [2, 4, 9, 9, 65536], P(None, None, None, None, ('dom', 'ply')), may hold values from -0.8984375 to 0.8984375
- cluster_ids: int32 [65536], P(('dom', 'ply')), may hold values from 0 to 1, as said below
- neighbour_faces: int32 [4, 65536], P(None, ('dom', 'ply')), may hold values from -1 to 511, as said below
- face_orient: int32 [4, 65536], P(None, ('dom', 'ply')), may hold values from 0 to 2
- plane_cut_faces: int32 [512, 1024], P(('dom', 'ply')), may hold values from -1 to 511, as said below
- thickness_faces: int32 [1024, 16], P(('dom', 'ply')), may hold values from 0 to 511, as said below
- stiffness: float32 [3, 35, 35], replicated, may hold values from -6 to 6, as said below
- trace_maps: float32 [4, 15, 35], replicated, may hold values from -1 to 1
- lift_maps: float32 [4, 35, 15], replicated, may hold values from -0.75 to 0.75
- face_rotations: float32 [3, 15, 15], replicated, may hold values from -1.5 to 1.5
Outputs:
- updated_dofs: float32 [9, 35, 65536], P(None, None, ('dom', 'ply'))
The draws below stay inside these ranges and needn't reach their ends.
Inputs may be any that keep to these rules, and one draw needn't show every extreme that they name: `cluster_ids`: 1 marks an element of the fine cluster, 0 one of the coarse cluster; at most 32 of one device's 128 elements are fine, and some device has exactly 32. `neighbour_faces`: row f, column e of device g's block is face n = f * 128 + e; its entry is the face number m of the same device that shares the face, and the entry of m names n back; -1 where the face is cut between devices or on the boundary. Column b * 8 + s of device g's row names a face number shared with the face at column a * 8 + s of the row of the device with dom index b and the same ply index (a being g's dom index), or -1 where both are unused; the used columns of a block come first; blocks are used only toward dom indices a + 1, a - 1, a + 3, a - 3 and a + 128 / 2 (modulo 128), each of these with one face or more; some blocks are full. A face number appears at most once among a device's plane_cut_faces, thickness_faces and nonnegative neighbour_faces entries. `thickness_faces`: all entries of one device are distinct face numbers; position k of the first row of a device is shared with position k of the second row of the device one ply index lower, position k of the second row with position k of the first row of the device one ply index higher; at the ends of the ply axis those faces are on the boundary. `stiffness`: entry [d, i, j] is zero unless basis function j has a higher polynomial degree than basis function i; the basis functions are ordered by degree, in groups of 1, 3, 6, 10 and 15.
All inputs are finite; a program needn't handle non-finite values.
Results may differ from the reference program's by a relative error of at most 0.00035.
Values sent between devices are 32-bit elements; how exact they have to be, the bound alone decides.
No kernel may reach another device: no remote copies, remote signals or barrier semaphores. Data moves between devices by JAX's collectives and lax.ppermute only.
A program may use at most 128 MiB of HBM per device.

```python
import jax
import jax.numpy as jnp
from jax import lax

QUANTS = 9
BASIS = 35
FACE_BASIS = 15
ORDER = 5
ELEM_DEV = 128
SLOT = 8
LAY = 16
FINE_MAX = 32
ELEMS = 65536
N_DOM = 128
N_PLY = 4
DEVICES = 512


def cut_layout(key):
    key_pairs, key_spot, key_order = jax.random.split(jax.random.fold_in(key, 5), 3)
    half_axis = N_DOM // 2
    pair_counts = jax.random.randint(key_pairs, (3, N_PLY, N_DOM), SLOT // 2 + 1, SLOT + 1)
    full_spot = jax.random.randint(key_spot, (), 0, N_DOM)
    pair_counts = pair_counts.at[0, :, full_spot].set(SLOT)
    onestep = pair_counts[0]
    threestep = pair_counts[1]
    across = jnp.take(pair_counts[2], jnp.arange(N_DOM) % half_axis, axis=1)
    domain = jnp.arange(N_DOM)
    distance = ((domain[None, :] - domain[:, None]) % N_DOM)[None, :, :]
    counts = jnp.where(distance == 1, onestep[:, :, None], 0) + jnp.where(distance == N_DOM - 1, jnp.roll(onestep, 1, axis=1)[:, :, None], 0) + jnp.where(distance == 3, threestep[:, :, None], 0) + jnp.where(distance == N_DOM - 3, jnp.roll(threestep, 3, axis=1)[:, :, None], 0) + jnp.where(distance == half_axis, across[:, :, None], 0)
    device_counts = jnp.transpose(counts, (1, 0, 2)).reshape(DEVICES, N_DOM).astype(jnp.int32)
    orders = jax.vmap(lambda sub_key: jax.random.permutation(sub_key, 4 * ELEM_DEV))(jax.random.split(key_order, DEVICES))

    def arrange(shuffled, per_peer):
        starts = jnp.cumsum(per_peer) - per_peer
        column = jnp.arange(N_DOM * SLOT)
        peer_index = column // SLOT
        within = column % SLOT
        in_use = within < per_peer[peer_index]
        plane_rows = jnp.where(in_use, shuffled[jnp.clip(2 * LAY + starts[peer_index] + within, 0, 4 * ELEM_DEV - 1)], -1)
        thick_rows = shuffled[:2 * LAY].reshape(2, LAY)
        first_free = 2 * LAY + jnp.sum(per_peer)
        positions = jnp.arange(4 * ELEM_DEV)
        partner = first_free + (positions - first_free ^ 1)
        linked = (positions >= first_free) & (partner < 4 * ELEM_DEV)
        values = jnp.where(linked, shuffled[jnp.clip(partner, 0, 4 * ELEM_DEV - 1)], -1)
        paired = jnp.full((4 * ELEM_DEV,), -1, jnp.int32).at[shuffled].set(values.astype(jnp.int32))
        return (paired, plane_rows.astype(jnp.int32), thick_rows.astype(jnp.int32))
    return jax.vmap(arrange)(orders, device_counts)


def draw_neighbour_faces(key, part):
    paired, plane_rows, thick_rows = cut_layout(key)
    return jnp.transpose(paired.reshape(DEVICES, 4, ELEM_DEV), (1, 0, 2)).reshape(4, ELEMS)


def draw_plane_cut_faces(key, part):
    paired, plane_rows, thick_rows = cut_layout(key)
    return plane_rows


def draw_thickness_faces(key, part):
    paired, plane_rows, thick_rows = cut_layout(key)
    return thick_rows.reshape(2 * DEVICES, LAY)


def draw_cluster_ids(key, part):
    key = jax.random.fold_in(key, 11)
    count_key, spot_key, order_key = jax.random.split(key, 3)
    counts = jax.random.randint(count_key, (DEVICES,), 1, max(FINE_MAX // 2, 2))
    busiest = jax.random.randint(spot_key, (), 0, DEVICES)
    counts = jnp.where(jnp.arange(DEVICES) == busiest, FINE_MAX, counts)
    shuffled = jax.vmap(lambda sub_key: jax.random.permutation(sub_key, ELEM_DEV))(jax.random.split(order_key, DEVICES))
    return (shuffled < counts[:, None]).astype(jnp.int32).reshape(-1)


def draw_stiffness(key, part):
    key = jax.random.fold_in(key, 17)
    basis_index = jnp.arange(BASIS)
    degree = (basis_index >= 1).astype(jnp.int32) + (basis_index >= 4) + (basis_index >= 10) + (basis_index >= 20)
    lowers = degree[:, None] < degree[None, :]
    entries = 0.8 * jax.random.normal(key, (3, BASIS, BASIS), jnp.float32)
    return jnp.where(lowers[None], entries, 0.0).astype(jnp.float32)


def set_ends(drawn, own_key, low, top_value):
    shape = drawn.shape
    spot = [jax.random.randint(jax.random.fold_in(own_key, axis), (), 0, shape[axis]) for axis in range(len(shape))]
    drawn = drawn.at[tuple(spot)].set(low)
    longest = shape.index(max(shape))
    spot[longest] = (spot[longest] + 1) % shape[longest]
    return drawn.at[tuple(spot)].set(top_value)


def shard_levels(own_key, extent, shards, low, top_value):
    def one(axis_at, parts):
        draws = jax.random.uniform(jax.random.fold_in(jax.random.fold_in(own_key, 6), axis_at), (parts,), jnp.float32, low / len(shards), top_value / len(shards))
        return jnp.repeat(jnp.exp(draws), extent[axis_at] // parts).reshape((-1,) + (1,) * (len(extent) - axis_at - 1))

    level = one(*shards[0])
    for cut in shards[1:]:
        level = level * one(*cut)
    return level


def gaussian(key, dims, deviation, bound, shards=(), held_as=jnp.bfloat16):
    gain = shard_levels(key, dims, shards, -0.22, 0.18) if shards else 1.0
    values = jax.random.normal(key, dims, jnp.float32) * deviation * gain
    return jnp.minimum(jnp.maximum(values, -bound), bound).astype(held_as)


def setup_inputs(seed: int = 0) -> dict:
    key_list = jax.random.split(jax.random.key(seed), 13)
    return {
        "state_dofs": gaussian(key_list[0], (QUANTS, BASIS, ELEMS), 1.0, 6.0, ((2, 512),), jnp.float32),
        "star_matrices": gaussian(key_list[1], (3, QUANTS, QUANTS, ELEMS), 0.06, 0.359375, ((3, 512),)),
        "flux_solvers": gaussian(key_list[2], (2, 4, QUANTS, QUANTS, ELEMS), 0.15, 0.8984375, ((4, 512),)),
        "cluster_ids": draw_cluster_ids(jax.random.fold_in(key_list[12], 71), 0),
        "neighbour_faces": draw_neighbour_faces(jax.random.fold_in(key_list[12], 71), 0),
        "face_orient": set_ends(jax.random.randint(key_list[5], (4, ELEMS), 0, 3), jax.random.fold_in(key_list[5], 1), 0, 2).astype(jnp.int32),
        "plane_cut_faces": draw_plane_cut_faces(jax.random.fold_in(key_list[12], 71), 0),
        "thickness_faces": draw_thickness_faces(jax.random.fold_in(key_list[12], 71), 0),
        "stiffness": draw_stiffness(jax.random.fold_in(key_list[12], 71), 0),
        "trace_maps": gaussian(key_list[9], (4, FACE_BASIS, BASIS), BASIS ** -0.5, 1.0, (), jnp.float32),
        "lift_maps": gaussian(key_list[10], (4, BASIS, FACE_BASIS), (4 * FACE_BASIS) ** -0.5, 0.75, (), jnp.float32),
        "face_rotations": gaussian(key_list[11], (3, FACE_BASIS, FACE_BASIS), FACE_BASIS ** -0.5, 1.5, (), jnp.float32),
    }


PRECISE = lax.Precision.HIGHEST


def derivative(values, star_mats, stiffness):
    stiffened = jnp.einsum("dij,pje->dpie", stiffness, values, precision=PRECISE)
    return -jnp.einsum("dqpe,dpie->qie", star_mats.astype(jnp.float32), stiffened, precision=PRECISE)


def taylor_integrals(values, star_mats, stiffness, intervals):
    totals = [jnp.zeros_like(values) for bounds in intervals]
    current = values
    factorial = 1.0
    for degree in range(ORDER):
        factorial = factorial * (degree + 1)
        for number in range(len(intervals)):
            weight = (intervals[number][1] ** (degree + 1) - intervals[number][0] ** (degree + 1)) / factorial
            totals[number] = totals[number] + weight * current
        if degree + 1 < ORDER:
            current = derivative(current, star_mats, stiffness)
    return totals


def volume(integral, star_mats, stiffness):
    stiffened = jnp.einsum("dji,pje->dpie", stiffness, integral, precision=PRECISE)
    return jnp.einsum("dqpe,dpie->qie", star_mats.astype(jnp.float32), stiffened, precision=PRECISE)


def face_values(integral, trace_maps):
    traced = jnp.einsum("fai,qie->qafe", trace_maps, integral, precision=PRECISE)
    return traced.reshape(QUANTS * FACE_BASIS, 4 * integral.shape[2])


def face_sources(neighbour, plane_list, thick_list, elements):
    all_faces = 4 * elements
    columns = plane_list.shape[0]
    layers = thick_list.shape[1]
    paired = neighbour.reshape(-1)
    sources = jnp.where(paired >= 0, paired, 0).astype(jnp.int32)
    present = paired >= 0
    plane_target = jnp.where(plane_list >= 0, plane_list, all_faces)
    sources = sources.at[plane_target].set(all_faces + jnp.arange(columns, dtype=jnp.int32), mode="drop")
    present = present.at[plane_target].set(True, mode="drop")
    thick_target = thick_list.reshape(-1)
    sources = sources.at[thick_target].set(all_faces + columns + jnp.arange(2 * layers, dtype=jnp.int32), mode="drop")
    present = present.at[thick_target].set(True, mode="drop")
    return sources, present


def outside_values(pool_cols, sources, present, face_orient, face_rotations):
    picked = jnp.take(pool_cols, sources, axis=1).reshape(QUANTS, FACE_BASIS, -1)
    turned = jnp.einsum("hab,qbn->hqan", face_rotations, picked, precision=PRECISE)
    choose = (face_orient.reshape(-1)[None, :] == jnp.arange(3, dtype=jnp.int32)[:, None]) & present[None, :]
    return jnp.sum(jnp.where(choose[:, None, None, :], turned, 0.0), axis=0)


def face_flux(own_side, outside, flux_solvers, lift_maps):
    elements = flux_solvers.shape[-1]
    inside = own_side.reshape(QUANTS, FACE_BASIS, 4, elements)
    beyond = outside.reshape(QUANTS, FACE_BASIS, 4, elements)
    solvers = flux_solvers.astype(jnp.float32)
    fluxes = jnp.einsum("fqpe,pafe->qafe", solvers[0], inside, precision=PRECISE) + jnp.einsum("fqpe,pafe->qafe", solvers[1], beyond, precision=PRECISE)
    return -jnp.einsum("fia,qafe->qie", lift_maps, fluxes, precision=PRECISE)


def peer_offsets():
    return (1, N_DOM - 1, 3, N_DOM - 3, N_DOM // 2)


def device_part(array, device, elements):
    return lax.dynamic_slice_in_dim(array, device * elements, elements, array.ndim - 1)


def sent_pieces(local, plane_list, thick_list, dom_index):
    all_faces = local.shape[1]
    outgoing = jnp.where(plane_list[None, :] >= 0, jnp.take(local, jnp.clip(plane_list, 0, all_faces - 1), axis=1), 0.0)
    blocks = jnp.stack([lax.dynamic_slice_in_dim(outgoing, ((dom_index + offset) % N_DOM) * SLOT, SLOT, 1) for offset in peer_offsets()])
    rim_rows = jnp.take(local, thick_list.reshape(-1), axis=1).reshape(local.shape[0], 2, LAY)
    return blocks, rim_rows


def deliver(blocks, rim_rows):
    blocks = blocks.reshape((N_DOM, N_PLY) + blocks.shape[1:])
    arrived = jnp.stack([jnp.roll(blocks[:, :, number], offset, axis=0) for number, offset in enumerate(peer_offsets())], axis=2)
    rim_rows = rim_rows.reshape((N_DOM, N_PLY) + rim_rows.shape[1:])
    nothing = jnp.zeros_like(rim_rows[:, :1, :, 0])
    from_below = jnp.concatenate([nothing, rim_rows[:, :-1, :, 1]], axis=1)
    from_above = jnp.concatenate([rim_rows[:, 1:, :, 0], nothing], axis=1)
    return (arrived.reshape((DEVICES,) + arrived.shape[2:]), from_below.reshape((DEVICES,) + from_below.shape[2:]), from_above.reshape((DEVICES,) + from_above.shape[2:]))


def build_pool(local, arrived, from_below, from_above, dom_index):
    received = jnp.zeros((local.shape[0], N_DOM * SLOT), local.dtype)
    for number, offset in enumerate(peer_offsets()):
        received = lax.dynamic_update_slice_in_dim(received, arrived[number], ((dom_index - offset) % N_DOM) * SLOT, 1)
    return jnp.concatenate([local, received, from_below, from_above], axis=1)


def reference(state_dofs, star_matrices, flux_solvers, cluster_ids, neighbour_faces, face_orient, plane_cut_faces, thickness_faces, stiffness, trace_maps, lift_maps, face_rotations):
    devices = jnp.arange(DEVICES, dtype=jnp.int32)

    def pieces(device):
        return (device_part(state_dofs, device, ELEM_DEV), device_part(star_matrices, device, ELEM_DEV), device_part(flux_solvers, device, ELEM_DEV), device_part(cluster_ids, device, ELEM_DEV) == 1, device_part(neighbour_faces, device, ELEM_DEV), device_part(face_orient, device, ELEM_DEV), lax.dynamic_index_in_dim(plane_cut_faces, device, 0, keepdims=False), lax.dynamic_slice_in_dim(thickness_faces, 2 * device, 2, 0))

    def first_round(device):
        device_data = pieces(device)
        early_part = taylor_integrals(device_data[0], device_data[1], stiffness, [(0.0, 0.5)])[0]
        return sent_pieces(face_values(early_part, trace_maps), device_data[6], device_data[7], device // N_PLY)

    def middle_state(device, device_data, arrived_first, below_first, above_first):
        initial, star_mats, solvers, is_fine, paired, orient, plane_list, thick_list = device_data
        early_part, coarse_late = taylor_integrals(initial, star_mats, stiffness, [(0.0, 0.5), (0.5, 1.0)])
        sources, present = face_sources(paired, plane_list, thick_list, ELEM_DEV)
        local_first = face_values(early_part, trace_maps)
        pool_first = build_pool(local_first, arrived_first, below_first, above_first, device // N_PLY)
        outside_first = outside_values(pool_first, sources, present, orient, face_rotations)
        middle = initial + volume(early_part, star_mats, stiffness) + face_flux(local_first, outside_first, solvers, lift_maps)
        return early_part, coarse_late, middle, outside_first, sources, present

    blocks, rim_rows = lax.map(first_round, devices)
    arrived, from_below, from_above = deliver(blocks, rim_rows)

    def second_round(inputs):
        device, arrived_first, below_first, above_first = inputs
        device_data = pieces(device)
        early_part, coarse_late, middle, outside_first, sources, present = middle_state(device, device_data, arrived_first, below_first, above_first)
        late_fine = taylor_integrals(middle, device_data[1], stiffness, [(0.0, 0.5)])[0]
        late_part = jnp.where(device_data[3], late_fine, coarse_late)
        blocks_late, rims_late = sent_pieces(face_values(late_part, trace_maps), device_data[6], device_data[7], device // N_PLY)
        return late_part, blocks_late, rims_late

    late_parts, blocks_late, rims_late = lax.map(second_round, (devices, arrived, from_below, from_above))
    arrived_late, below_late, above_late = deliver(blocks_late, rims_late)

    def final_round(inputs):
        device, arrived_first, below_first, above_first, late_part, arrived_second, below_second, above_second = inputs
        device_data = pieces(device)
        initial, star_mats, solvers, is_fine = device_data[0], device_data[1], device_data[2], device_data[3]
        early_part, coarse_late, middle, outside_first, sources, present = middle_state(device, device_data, arrived_first, below_first, above_first)
        local_late = face_values(late_part, trace_maps)
        pool_late = build_pool(local_late, arrived_second, below_second, above_second, device // N_PLY)
        outside_late = outside_values(pool_late, sources, present, device_data[5], face_rotations)
        fine_result = middle + volume(late_part, star_mats, stiffness) + face_flux(local_late, outside_late, solvers, lift_maps)
        whole_step = early_part + late_part
        coarse_result = initial + volume(whole_step, star_mats, stiffness) + face_flux(face_values(whole_step, trace_maps), outside_first + outside_late, solvers, lift_maps)
        return jnp.where(is_fine, fine_result, coarse_result)

    results = lax.map(final_round, (devices, arrived, from_below, from_above, late_parts, arrived_late, below_late, above_late))
    return jnp.moveaxis(results, 0, 2).reshape(QUANTS, BASIS, DEVICES * results.shape[3])
```

```python
import jax
import jax.numpy as jnp
from jax import lax
from jax.experimental import pallas as pl
from jax.experimental.pallas import tpu as pltpu
from jax.sharding import PartitionSpec as P

F32, BF16 = jnp.float32, jnp.bfloat16
Q, B, A, ORDER = 9, 35, 15, 5
E = 128
PAD = 48
AP = 16
SLOT, LAY = 8, 16
CUTS = 5 * SLOT + 2 * LAY
CP = 80
WIDE = Q * E
ALL = 4 * E

EARLY = [0.5 ** (k + 1) for k in range(ORDER)]
LATE = [1.0 - 0.5 ** (k + 1) for k in range(ORDER)]
FACT = [1.0, 2.0, 6.0, 24.0, 120.0]
STEPS = [(24, 48), (16, 32), (8, 16), (8, 16)]


def dot(a, b):
    return jnp.dot(a, b, preferred_element_type=F32)


def halves(x):
    top = x.astype(BF16)
    return top, (x - top.astype(F32)).astype(BF16)


def tripled(a):
    top = a.astype(BF16).astype(F32)
    return jnp.concatenate([top, top, a - top], axis=1).astype(BF16)


def padded(a, rows, cols):
    r, c = a.shape
    if c < cols:
        a = jnp.concatenate([a, jnp.zeros((r, cols - c), a.dtype)], axis=1)
    if r < rows:
        a = jnp.concatenate([a, jnp.zeros((rows - r, cols), a.dtype)], axis=0)
    return a


def lanes(p):
    return slice(p * E, (p + 1) * E)


def put_stack(ref, rows, p, value):
    top, rest = halves(value)
    ref[0:rows, lanes(p)] = top
    ref[rows : 2 * rows, lanes(p)] = rest
    ref[2 * rows : 3 * rows, lanes(p)] = top


def stiff_rows(stiffness, rows, cols):
    blocks = [
        tripled(padded(stiffness[d], PAD, PAD)[:rows, :cols]).astype(F32) for d in range(3)
    ]
    return jnp.concatenate(blocks, axis=0).astype(BF16)


def trace_rows(trace_maps):
    blocks = [tripled(padded(trace_maps[:, f, :], AP, PAD)).astype(F32) for f in range(4)]
    return jnp.concatenate(blocks, axis=0).astype(BF16)


def volume_rows(stiffness):
    blocks = [tripled(padded(stiffness[d].T, 40, PAD)).astype(F32) for d in range(3)]
    return jnp.concatenate(blocks, axis=0).astype(BF16)


def lift_rows(lift_maps):
    return tripled(jnp.concatenate([padded(lift_maps[:, f, :].T, 40, AP) for f in range(4)], axis=1))


def turn_rows(face_rotations):
    blocks = [tripled(padded(face_rotations[h], AP, AP)).astype(F32) for h in range(3)]
    return jnp.concatenate(blocks, axis=0).astype(BF16)


def widen(source, target, blocks):
    for n in range(blocks):
        target[n] = source[n].astype(F32)


def star_apply(y, stars, rows):
    def one(p, total):
        total = list(total)
        at = pl.ds(pl.multiple_of(p * E, E), E)
        for d in range(3):
            value = y[d * rows : (d + 1) * rows, at]
            for q in range(Q):
                total[q] = total[q] + stars[q * Q + p, d : d + 1, :] * value
        return tuple(total)

    return lax.fori_loop(0, Q, one, tuple(jnp.zeros((rows, E), F32) for _ in range(Q)))


def taylor(first, steps, stars, x, y, add):
    values = [first[q] for q in range(Q)]
    for k, (rows, reads) in enumerate(STEPS):
        for p in range(Q):
            put_stack(x, reads, p, padded(values[p], reads, E))
        y[0 : 3 * rows, :] = dot(steps[k][...], x[0 : 3 * reads, :])
        values = star_apply(y, stars, rows)
        for q in range(Q):
            add(k + 1, q, rows, values[q])


def far_first(count):
    return (count // 2, count - 3, count - 1, 3, 1)


def shared_faces(plane, thick):
    dom, ply = lax.axis_index("dom"), lax.axis_index("ply")
    count = lax.axis_size("dom")
    odd, high = lax.rem(dom, 2), lax.rem(ply, 2)
    sub = lax.broadcasted_iota(jnp.int32, (SLOT, E), 0)
    groups = []
    for step in far_first(count):
        peer = lax.rem(dom + jnp.where(odd == 0, step, count - step), count)
        groups.append(lambda s, at=peer * SLOT: plane[0, at + s])
    for row in (1 - high, high):
        for half in (0, SLOT):
            groups.append(lambda s, row=row, half=half: thick[row, half + s])
    columns = []
    for face in groups:
        column = jnp.full((SLOT, E), -1, jnp.int32)
        for s in range(SLOT):
            column = jnp.where(sub == s, face(s), column)
        columns.append(column)
    columns.append(jnp.full((SLOT, E), -1, jnp.int32))
    return jnp.concatenate(columns, axis=0)


def pick_shared(plane, thick, hot):
    column = shared_faces(plane, thick)
    lane = lax.broadcasted_iota(jnp.int32, (CP, E), 1)
    for f in range(4):
        hot[:, lanes(f)] = jnp.where(column == lane + f * E, 1.0, 0.0).astype(BF16)


def send_traces(s, hot, l, outs):
    for q in range(Q):
        for f in range(4):
            value = s[f * AP : (f + 1) * AP, lanes(q)]
            for part in range(3):
                piece = value.astype(BF16)
                value = value - piece.astype(F32)
                l[part * Q * AP + q * AP : part * Q * AP + (q + 1) * AP, lanes(f)] = piece
    total = None
    for part in (2, 1, 0):
        piece = lax.dot_general(
            hot[...],
            l[part * Q * AP : (part + 1) * Q * AP, :],
            (((1,), (1,)), ((), ())),
            preferred_element_type=F32,
        )
        total = piece if total is None else total + piece
    at = 0
    for out in outs:
        out[...] = total[at : at + out.shape[0]]
        at += out.shape[0]


def first_kernel(state, star, stiffness, trace_maps, plane, thick,
                 x_out, s_out, coarse, hot, stars, step1, step2, step3, step4, traces, *rest):
    sends = rest[:7]
    (stiff_here, trace_here, star_here, state_here, plane_here, thick_here, sems,
     first, early, x, y, l) = rest[7:]
    here = (stiff_here, trace_here, star_here, state_here, plane_here, thick_here)
    there = (stiffness, trace_maps, star, state, plane, thick)
    copies = [
        pltpu.make_async_copy(source, target, sems.at[n])
        for n, (source, target) in enumerate(zip(there, here))
    ]
    for copy in copies:
        copy.start()
    first[...] = jnp.zeros_like(first)
    copies[0].wait()
    steps = (step1, step2, step3, step4)
    for step, (rows, reads) in zip(steps, STEPS):
        step[...] = stiff_rows(stiff_here, rows, reads)
    copies[1].wait()
    traces[...] = trace_rows(trace_here)
    for copy in copies[2:]:
        copy.wait()
    pick_shared(plane_here, thick_here, hot)
    widen(star_here, stars, Q * Q)
    first[:, 0:B, :] = state_here[...]
    early[...] = first[...] * EARLY[0]
    coarse[...] = first[:, 0:40, :] * LATE[0]

    def add(k, q, rows, value):
        sign = -1.0 if k % 2 else 1.0
        early[q, 0:rows, :] = early[q, 0:rows, :] + value * (sign * EARLY[k] / FACT[k])
        coarse[q, 0:rows, :] = coarse[q, 0:rows, :] + value * (sign * LATE[k] / FACT[k])

    taylor(first, steps, stars, x, y, add)
    for p in range(Q):
        put_stack(x_out, PAD, p, early[p])
    s_out[...] = dot(traces[...], x_out[...])
    send_traces(s_out, hot, l, sends)


def own_part(base, x, s, stars, solvers, volumes, same, held, own, picked, y, l):
    for q in range(Q):
        for f in range(4):
            top, rest = halves(s[f * AP : (f + 1) * AP, lanes(q)])
            l[q * AP : (q + 1) * AP, lanes(f)] = top
            l[Q * AP + q * AP : Q * AP + (q + 1) * AP, lanes(f)] = rest
    picked[...] = dot(l[...], same[...])
    y[...] = dot(volumes[...], x[...])
    sums = star_apply(y, stars, 40)
    for q in range(Q):
        held[q] = base(q) + sums[q]
    fluxes(solvers, 0, s, own, None)


def fluxes(solvers, side, values, g, before):
    for f in range(4):
        rows = slice(f * AP, (f + 1) * AP)

        def face(p, total):
            total = list(total)
            at = pl.ds(pl.multiple_of(p * E, E), E)
            value = values[rows, at]
            for q in range(Q):
                total[q] = total[q] + solvers[(side * Q + q) * Q + p, f : f + 1, :] * value
            return tuple(total)

        start = [jnp.zeros((AP, E), F32) if before is None else before[rows, lanes(q)] for q in range(Q)]
        total = lax.fori_loop(0, Q, face, tuple(start))
        for q in range(Q):
            g[rows, lanes(q)] = total[q]


def early_own_kernel(state, x, s, stars, flux, neighbour, stiffness, lift_maps, rotations,
                     held, own, picked, solvers, same, volumes, lifts, turns, padded_state, y, l):
    widen(flux, solvers, 2 * Q * Q)
    sub = lax.broadcasted_iota(jnp.int32, (ALL, E), 0)
    for f in range(4):
        same[:, lanes(f)] = jnp.where(sub == neighbour[f : f + 1, :], 1.0, 0.0).astype(BF16)
    volumes[...] = volume_rows(stiffness)
    lifts[...] = lift_rows(lift_maps)
    turns[...] = turn_rows(rotations)
    padded_state[...] = jnp.zeros_like(padded_state)
    padded_state[:, 0:B, :] = state[...]
    own_part(lambda q: padded_state[q], x, s, stars, solvers, volumes, same, held, own, picked, y, l)


def late_own_kernel(middle, x, s, stars, solvers, volumes, same, held, own, picked, y, l):
    own_part(lambda q: middle[q], x, s, stars, solvers, volumes, same, held, own, picked, y, l)


def finished(held, own, picked, arrived, hot, orient, solvers, lifts, turns, turned_in, o, g):
    landed = jnp.concatenate(
        [ref[...] for ref in arrived] + [jnp.zeros((CP - CUTS, Q * AP), F32)], axis=0
    )
    both = [
        picked[part * Q * AP : (part + 1) * Q * AP, :]
        + lax.dot_general(
            piece, hot[...], (((0,), (0,)), ((), ())), preferred_element_type=F32
        )
        for part, piece in enumerate(halves(landed))
    ]
    for q in range(Q):
        cols = slice(q * ALL, (q + 1) * ALL)
        top = both[0][q * AP : (q + 1) * AP].astype(BF16)
        turned_in[0:AP, cols] = top
        turned_in[AP : 2 * AP, cols] = both[1][q * AP : (q + 1) * AP].astype(BF16)
        turned_in[2 * AP : 3 * AP, cols] = top
    for q in range(Q):
        turned = dot(turns[...], turned_in[:, q * ALL : (q + 1) * ALL])
        for f in range(4):
            way = orient[f : f + 1, :]
            o[f * AP : (f + 1) * AP, lanes(q)] = jnp.where(
                way == 0,
                turned[0:AP, lanes(f)],
                jnp.where(way == 1, turned[AP : 2 * AP, lanes(f)], turned[2 * AP : 3 * AP, lanes(f)]),
            )
    fluxes(solvers, 1, o, g, own)
    results = []
    for q in range(Q):
        top, rest = halves(g[:, lanes(q)])
        results.append(held[q] - dot(lifts[...], jnp.concatenate([top, rest, top], axis=0)))
    return results


def middle_kernel(held, own, picked, coarse, hot, orient, cluster, stars, solvers, lifts, turns,
                  step1, step2, step3, step4, traces, *rest):
    arrived, (middle, x_out, s_out), sends = rest[:7], rest[7:10], rest[10:17]
    first, late, x, y, l, turned_in, o, g = rest[17:]
    values = finished(held, own, picked, arrived, hot, orient, solvers, lifts, turns, turned_in, o, g)
    for q in range(Q):
        first[q] = padded(values[q], PAD, E)
        middle[q] = values[q]
        late[q] = first[q] * EARLY[0]

    def add(k, q, rows, value):
        sign = -1.0 if k % 2 else 1.0
        late[q, 0:rows, :] = late[q, 0:rows, :] + value * (sign * EARLY[k] / FACT[k])

    taylor(first, (step1, step2, step3, step4), stars, x, y, add)
    fine = cluster[...] == 1
    for q in range(Q):
        late[q, 0:40, :] = jnp.where(fine, late[q, 0:40, :], coarse[q])
        put_stack(x_out, PAD, q, late[q])
    s_out[...] = dot(traces[...], x_out[...])
    send_traces(s_out, hot, l, sends)


def last_kernel(held, own, picked, hot, orient, solvers, lifts, turns, *rest):
    arrived, out, (turned_in, o, g) = rest[:7], rest[7], rest[8:]
    values = finished(held, own, picked, arrived, hot, orient, solvers, lifts, turns, turned_in, o, g)
    for q in range(Q):
        out[q] = values[q][0:B]


def shape(dims, kind=F32):
    return jax.ShapeDtypeStruct(dims, kind)


SENDS = [(SLOT, Q * AP)] * 5 + [(LAY, Q * AP)] * 2
PADDED = pltpu.VMEM((Q, PAD, E), F32)
X = pltpu.VMEM((3 * PAD, WIDE), BF16)
Y = pltpu.VMEM((120, WIDE), F32)
TWO = pltpu.VMEM((2 * Q * AP, ALL), BF16)
THREE = pltpu.VMEM((3 * Q * AP, ALL), BF16)
TURNED = pltpu.VMEM((3 * AP, Q * ALL), BF16)
SIDE = pltpu.VMEM((4 * AP, WIDE), F32)


def call(kernel, operands, outs, scratch, flops, memory=pltpu.VMEM, limit=40):
    vmem, source = pl.BlockSpec(memory_space=pltpu.VMEM), pl.BlockSpec(memory_space=memory)
    return pl.pallas_call(
        kernel,
        out_shape=outs,
        in_specs=[source] * len(operands),
        out_specs=jax.tree.map(lambda _: vmem, outs),
        scratch_shapes=scratch,
        compiler_params=pltpu.CompilerParams(vmem_limit_bytes=limit * 1024 * 1024),
        cost_estimate=pl.CostEstimate(flops=flops, bytes_accessed=2_000_000, transcendentals=0),
    )(*operands)


def exchange(blocks):
    count, layers = lax.axis_size("dom"), lax.axis_size("ply")
    landed = []
    for step, block in zip(far_first(count), blocks):
        pairs = []
        for even in range(0, count, 2):
            other = (even + step) % count
            pairs += [(even, other)] + ([(other, even)] if step % 2 else [])
        if step % 2 == 0:
            pairs = [(i, (i + step) % count) for i in range(count)]
        landed.append(lax.ppermute(block, "dom", pairs))
    for start, block in zip((0, 1), blocks[5:]):
        pairs = []
        for low in range(start, layers - 1, 2):
            pairs += [(low, low + 1), (low + 1, low)]
        landed.append(lax.ppermute(block, "ply", pairs))
    return landed


def body(state, star, flux, cluster, neighbour, orient, plane, thick,
         stiffness, trace_maps, lift_maps, rotations):
    star = star.transpose(1, 2, 0, 3).reshape(Q * Q, 3, E)
    flux = flux.transpose(0, 2, 3, 1, 4).reshape(2 * Q * Q, 4, E)
    trace_maps = trace_maps.transpose(1, 0, 2)
    lift_maps = lift_maps.transpose(2, 0, 1)
    cluster = cluster.reshape(1, E)
    kept = [shape((3 * PAD, WIDE), BF16), shape((4 * AP, WIDE)), shape((Q, 40, E))]
    sends = [shape(dims) for dims in SENDS]
    wide = shape((Q * Q, 3, E))
    products = [shape((3 * rows, 3 * reads), BF16) for rows, reads in STEPS]
    products.append(shape((4 * AP, 3 * PAD), BF16))
    own_outs = [kept[2], kept[1], shape((2 * Q * AP, ALL))]
    x_early, s_early, coarse, hot, stars, *rest = call(
        first_kernel, (state, star, stiffness, trace_maps, plane, thick),
        kept + [shape((CP, ALL), BF16), wide] + products + sends,
        [
            pltpu.VMEM(stiffness.shape, F32),
            pltpu.VMEM(trace_maps.shape, F32),
            pltpu.VMEM(star.shape, BF16),
            pltpu.VMEM(state.shape, F32),
            pltpu.SMEM(plane.shape, jnp.int32),
            pltpu.SMEM(thick.shape, jnp.int32),
            pltpu.SemaphoreType.DMA((6,)),
            PADDED, PADDED, X, Y, THREE,
        ],
        100_000_000, pltpu.HBM, 60,
    )
    steps, out_early = rest[:5], rest[5:]
    in_early = exchange(out_early)
    held, own, picked, solvers, same, volumes, lifts, turns = call(
        early_own_kernel,
        (state, x_early, s_early, stars, flux, neighbour, stiffness, lift_maps, rotations),
        own_outs + [
            shape((2 * Q * Q, 4, E)), shape((ALL, ALL), BF16), shape((120, 3 * PAD), BF16),
            shape((40, 12 * AP), BF16), shape((3 * AP, 3 * AP), BF16),
        ],
        [pltpu.VMEM((Q, 40, E), F32), Y, TWO], 200_000_000,
    )
    middle, x_late, s_late, *out_late = call(
        middle_kernel,
        (held, own, picked, coarse, hot, orient, cluster, stars, solvers, lifts, turns, *steps,
         *in_early),
        [kept[2], kept[0], kept[1]] + sends,
        [PADDED, PADDED, X, Y, THREE, TURNED, SIDE, SIDE], 200_000_000,
    )
    in_late = exchange(out_late)
    held, own, picked = call(
        late_own_kernel, (middle, x_late, s_late, stars, solvers, volumes, same), own_outs,
        [Y, TWO], 200_000_000,
    )
    return call(
        last_kernel, (held, own, picked, hot, orient, solvers, lifts, turns, *in_late),
        shape((Q, B, E)), [TURNED, SIDE, SIDE], 100_000_000,
    )


def solution(mesh):
    both = ("dom", "ply")
    in_specs = (
        P(None, None, both),
        P(None, None, None, both),
        P(None, None, None, None, both),
        P(both),
        P(None, both),
        P(None, both),
        P(both, None),
        P(both, None),
        P(),
        P(),
        P(),
        P(),
    )
    return jax.shard_map(
        body, mesh=mesh, in_specs=in_specs, out_specs=P(None, None, both), check_vma=False
    )
```

```python
import jax
import jax.numpy as jnp
from jax import lax
from jax.experimental import pallas as pl
from jax.experimental.pallas import tpu as pltpu
from jax.sharding import PartitionSpec as P

F32, BF16 = jnp.float32, jnp.bfloat16
Q, B, A, ORDER = 9, 35, 15, 5
E = 128
PAD = 48
AP = 16
SLOT, LAY = 8, 16
CUTS = 5 * SLOT + 2 * LAY
CP = 80
WIDE = Q * E
ALL = 4 * E

EARLY = [0.5 ** (k + 1) for k in range(ORDER)]
LATE = [1.0 - 0.5 ** (k + 1) for k in range(ORDER)]
FACT = [1.0, 2.0, 6.0, 24.0, 120.0]
STEPS = [(24, 48), (16, 32), (8, 16), (8, 16)]


def dot(a, b):
    return jnp.dot(a, b, preferred_element_type=F32)


def halves(x):
    top = x.astype(BF16)
    return top, (x - top.astype(F32)).astype(BF16)


def tripled(a):
    top = a.astype(BF16).astype(F32)
    return jnp.concatenate([top, top, a - top], axis=1).astype(BF16)


def padded(a, rows, cols):
    r, c = a.shape
    if c < cols:
        a = jnp.concatenate([a, jnp.zeros((r, cols - c), a.dtype)], axis=1)
    if r < rows:
        a = jnp.concatenate([a, jnp.zeros((rows - r, cols), a.dtype)], axis=0)
    return a


def lanes(p):
    return slice(p * E, (p + 1) * E)


def put_stack(ref, rows, p, value):
    top, rest = halves(value)
    ref[0:rows, lanes(p)] = top
    ref[rows : 2 * rows, lanes(p)] = rest
    ref[2 * rows : 3 * rows, lanes(p)] = top


def stiff_rows(stiffness, rows, cols):
    blocks = [
        tripled(padded(stiffness[d], PAD, PAD)[:rows, :cols]).astype(F32) for d in range(3)
    ]
    return jnp.concatenate(blocks, axis=0).astype(BF16)


def trace_rows(trace_maps):
    blocks = [tripled(padded(trace_maps[f], AP, PAD)).astype(F32) for f in range(4)]
    return jnp.concatenate(blocks, axis=0).astype(BF16)


def volume_rows(stiffness):
    blocks = [tripled(padded(stiffness[d].T, 40, PAD)).astype(F32) for d in range(3)]
    return jnp.concatenate(blocks, axis=0).astype(BF16)


def lift_rows(lift_maps):
    return tripled(jnp.concatenate([padded(lift_maps[:, f, :].T, 40, AP) for f in range(4)], axis=1))


def turn_rows(face_rotations):
    blocks = [tripled(padded(face_rotations[h], AP, AP)).astype(F32) for h in range(3)]
    return jnp.concatenate(blocks, axis=0).astype(BF16)


def widen(source, target, blocks):
    for n in range(blocks):
        target[n] = source[n].astype(F32)


def star_apply(y, stars, rows):
    def one(p, total):
        total = list(total)
        at = pl.ds(pl.multiple_of(p * E, E), E)
        for d in range(3):
            value = y[d * rows : (d + 1) * rows, at]
            for q in range(Q):
                total[q] = total[q] + stars[q * Q + p, d : d + 1, :] * value
        return tuple(total)

    start = tuple(jnp.zeros((rows, E), F32) for _ in range(Q))
    return lax.fori_loop(0, Q, one, start, unroll=Q if rows < 40 else 3)


def taylor(first, steps, stars, x, y, add):
    values = [first[q] for q in range(Q)]
    for k, (rows, reads) in enumerate(STEPS):
        for p in range(Q):
            put_stack(x, reads, p, padded(values[p], reads, E))
        y[0 : 3 * rows, :] = dot(steps[k][...], x[0 : 3 * reads, :])
        values = star_apply(y, stars, rows)
        for q in range(Q):
            add(k + 1, q, rows, values[q])


def far_steps(count):
    return (count - 3, count // 2)


def near_steps(count):
    return (count - 1, 3, 1)


def shared_faces(plane, thick):
    dom, ply = lax.axis_index("dom"), lax.axis_index("ply")
    count = lax.axis_size("dom")
    odd, high = lax.rem(dom, 2), lax.rem(ply, 2)
    sub = lax.broadcasted_iota(jnp.int32, (SLOT, E), 0)
    def plane_group(step):
        peer = lax.rem(dom + jnp.where(odd == 0, step, count - step), count)
        return lambda s: plane[0, peer * SLOT + s]

    groups = [plane_group(step) for step in far_steps(count)]
    for row in (1 - high, high):
        for half in (0, SLOT):
            groups.append(lambda s, row=row, half=half: thick[row, half + s])
    groups += [plane_group(step) for step in near_steps(count)]
    columns = []
    for face in groups:
        column = jnp.full((SLOT, E), -1, jnp.int32)
        for s in range(SLOT):
            column = jnp.where(sub == s, face(s), column)
        columns.append(column)
    columns.append(jnp.full((SLOT, E), -1, jnp.int32))
    return jnp.concatenate(columns, axis=0)


def pick_shared(plane, thick, hot):
    column = shared_faces(plane, thick)
    lane = lax.broadcasted_iota(jnp.int32, (CP, E), 1)
    for f in range(4):
        hot[:, lanes(f)] = jnp.where(column == lane + f * E, 1.0, 0.0).astype(BF16)


def send_traces(s, hot, l, outs):
    split_traces(s, l)
    total = None
    for part in (1, 0):
        piece = lax.dot_general(
            hot[...],
            l[part * Q * AP : (part + 1) * Q * AP, :],
            (((1,), (1,)), ((), ())),
            preferred_element_type=F32,
        )
        total = piece if total is None else total + piece
    at = 0
    for out in outs[:-1]:
        out[...] = total[at : at + out.shape[0]]
        at += out.shape[0]
    outs[-1][...] = jnp.zeros_like(outs[-1])
    outs[-1][0:SLOT] = total[at : at + SLOT]


def split_traces(s, l):
    for q in range(Q):
        for f in range(4):
            top, rest = halves(s[f * AP : (f + 1) * AP, lanes(q)])
            l[q * AP : (q + 1) * AP, lanes(f)] = top
            l[Q * AP + q * AP : Q * AP + (q + 1) * AP, lanes(f)] = rest


def first_kernel(state, stars, stiffness, trace_maps, plane, thick, neighbour, orient, cluster,
                 x_out, s_out, coarse, hot, marks, l, step1, step2, step3, step4, traces, *rest):
    sends, (first, early, x, y) = rest[:7], rest[7:]
    steps = (step1, step2, step3, step4)
    for step, (rows, reads) in zip(steps, STEPS):
        step[...] = stiff_rows(stiffness, rows, reads)
    traces[...] = trace_rows(trace_maps)
    pick_shared(plane, thick, hot)
    marks[0:4] = neighbour[...]
    marks[4:8] = orient[...]
    marks[8:9] = cluster[...]
    first[...] = jnp.zeros_like(first)
    first[:, 0:B, :] = state[...]
    early[...] = first[...] * EARLY[0]
    coarse[...] = first[:, 0:40, :] * LATE[0]

    def add(k, q, rows, value):
        sign = -1.0 if k % 2 else 1.0
        early[q, 0:rows, :] = early[q, 0:rows, :] + value * (sign * EARLY[k] / FACT[k])
        coarse[q, 0:rows, :] = coarse[q, 0:rows, :] + value * (sign * LATE[k] / FACT[k])

    taylor(first, steps, stars, x, y, add)
    for p in range(Q):
        put_stack(x_out, PAD, p, early[p])
    s_out[...] = dot(traces[...], x_out[...])
    send_traces(s_out, hot, l, sends)


def own_part(base, x, s, l, stars, solvers, volumes, same, held, own, picked, y):
    picked[...] = dot(l[...], same[...])
    y[...] = dot(volumes[...], x[...])
    sums = star_apply(y, stars, 40)
    for q in range(Q):
        held[q] = base(q) + sums[q]
    fluxes(solvers, 0, s, own, None)


def fluxes(solvers, side, values, g, before):
    for f in range(4):
        rows = slice(f * AP, (f + 1) * AP)

        def face(p, total):
            total = list(total)
            at = pl.ds(pl.multiple_of(p * E, E), E)
            value = values[rows, at]
            for q in range(Q):
                total[q] = total[q] + solvers[(side * Q + q) * Q + p, f : f + 1, :] * value
            return tuple(total)

        start = [jnp.zeros((AP, E), F32) if before is None else before[rows, lanes(q)] for q in range(Q)]
        total = lax.fori_loop(0, Q, face, tuple(start), unroll=Q)
        for q in range(Q):
            g[rows, lanes(q)] = total[q]


def early_own_kernel(state, x, s, l, stars, flux, marks, stiffness, lift_maps, rotations,
                     held, own, picked, solvers, same, volumes, lifts, turns, padded_state, y):
    widen(flux, solvers, 2 * Q * Q)
    sub = lax.broadcasted_iota(jnp.int32, (ALL, E), 0)
    for f in range(4):
        same[:, lanes(f)] = jnp.where(sub == marks[f : f + 1, :], 1.0, 0.0).astype(BF16)
    volumes[...] = volume_rows(stiffness)
    lifts[...] = lift_rows(lift_maps)
    turns[...] = turn_rows(rotations)
    padded_state[...] = jnp.zeros_like(padded_state)
    padded_state[:, 0:B, :] = state[...]
    own_part(lambda q: padded_state[q], x, s, l, stars, solvers, volumes, same, held, own, picked, y)


def late_own_kernel(middle, x, s, l, stars, solvers, volumes, same, held, own, picked, y):
    own_part(lambda q: middle[q], x, s, l, stars, solvers, volumes, same, held, own, picked, y)


def finished(held, own, picked, arrived, hot, marks, solvers, lifts, turns, turned_in, o, g):
    landed = jnp.concatenate(
        [ref[...] for ref in arrived[:-1]]
        + [arrived[-1][0:SLOT], jnp.zeros((CP - CUTS, Q * AP), F32)], axis=0
    )
    both = [
        picked[part * Q * AP : (part + 1) * Q * AP, :]
        + lax.dot_general(
            piece, hot[...], (((0,), (0,)), ((), ())), preferred_element_type=F32
        )
        for part, piece in enumerate(halves(landed))
    ]
    for q in range(Q):
        cols = slice(q * ALL, (q + 1) * ALL)
        top = both[0][q * AP : (q + 1) * AP].astype(BF16)
        turned_in[0:AP, cols] = top
        turned_in[AP : 2 * AP, cols] = both[1][q * AP : (q + 1) * AP].astype(BF16)
        turned_in[2 * AP : 3 * AP, cols] = top
    for q in range(Q):
        turned = dot(turns[...], turned_in[:, q * ALL : (q + 1) * ALL])
        for f in range(4):
            way = marks[4 + f : 5 + f, :]
            o[f * AP : (f + 1) * AP, lanes(q)] = jnp.where(
                way == 0,
                turned[0:AP, lanes(f)],
                jnp.where(way == 1, turned[AP : 2 * AP, lanes(f)], turned[2 * AP : 3 * AP, lanes(f)]),
            )
    fluxes(solvers, 1, o, g, own)
    results = []
    for q in range(Q):
        top, rest = halves(g[:, lanes(q)])
        results.append(held[q] - dot(lifts[...], jnp.concatenate([top, rest, top], axis=0)))
    return results


def middle_kernel(held, own, picked, coarse, hot, marks, stars, solvers, lifts, turns,
                  step1, step2, step3, step4, traces, *rest):
    arrived, (middle, x_out, s_out, l), sends = rest[:7], rest[7:11], rest[11:18]
    first, late, x, y, turned_in, o, g = rest[18:]
    values = finished(held, own, picked, arrived, hot, marks, solvers, lifts, turns, turned_in, o, g)
    for q in range(Q):
        first[q] = padded(values[q], PAD, E)
        middle[q] = values[q]
        late[q] = first[q] * EARLY[0]

    def add(k, q, rows, value):
        sign = -1.0 if k % 2 else 1.0
        late[q, 0:rows, :] = late[q, 0:rows, :] + value * (sign * EARLY[k] / FACT[k])

    taylor(first, (step1, step2, step3, step4), stars, x, y, add)
    fine = marks[8:9, :] == 1
    for q in range(Q):
        late[q, 0:40, :] = jnp.where(fine, late[q, 0:40, :], coarse[q])
        put_stack(x_out, PAD, q, late[q])
    s_out[...] = dot(traces[...], x_out[...])
    send_traces(s_out, hot, l, sends)


def last_kernel(held, own, picked, hot, marks, solvers, lifts, turns, *rest):
    arrived, out, (turned_in, o, g) = rest[:7], rest[7], rest[8:]
    values = finished(held, own, picked, arrived, hot, marks, solvers, lifts, turns, turned_in, o, g)
    for q in range(Q):
        out[q] = values[q][0:B]


def shape(dims, kind=F32):
    return jax.ShapeDtypeStruct(dims, kind)


CORE_ROWS = 24
SENDS = (
    [(SLOT, Q * AP)] * 2 + [(LAY, Q * AP)] * 2 + [(SLOT, Q * AP)] * 2 + [(CORE_ROWS, Q * AP)]
)
PADDED = pltpu.VMEM((Q, PAD, E), F32)
X = pltpu.VMEM((3 * PAD, WIDE), BF16)
Y = pltpu.VMEM((120, WIDE), F32)
TURNED = pltpu.VMEM((3 * AP, Q * ALL), BF16)
SIDE = pltpu.VMEM((4 * AP, WIDE), F32)


def call(kernel, operands, outs, scratch, flops, scalars=()):
    vmem, smem = pl.BlockSpec(memory_space=pltpu.VMEM), pl.BlockSpec(memory_space=pltpu.SMEM)
    return pl.pallas_call(
        kernel,
        out_shape=outs,
        in_specs=[smem if n in scalars else vmem for n in range(len(operands))],
        out_specs=jax.tree.map(lambda _: vmem, outs),
        scratch_shapes=scratch,
        compiler_params=pltpu.CompilerParams(vmem_limit_bytes=40 * 1024 * 1024),
        cost_estimate=pl.CostEstimate(flops=flops, bytes_accessed=2_000_000, transcendentals=0),
    )(*operands)


def exchange(blocks):
    count, layers = lax.axis_size("dom"), lax.axis_size("ply")

    def along_dom(step, block):
        if step % 2 == 0:
            pairs = [(i, (i + step) % count) for i in range(count)]
        else:
            pairs = []
            for even in range(0, count, 2):
                other = (even + step) % count
                pairs += [(even, other), (other, even)]
        return lax.ppermute(block, "dom", pairs)

    def along_ply(start, block):
        pairs = []
        for low in range(start, layers - 1, 2):
            pairs += [(low, low + 1), (low + 1, low)]
        return lax.ppermute(block, "ply", pairs)

    return (
        [along_dom(step, block) for step, block in zip(far_steps(count), blocks)]
        + [along_ply(start, block) for start, block in zip((0, 1), blocks[2:])]
        + [along_dom(step, block) for step, block in zip(near_steps(count), blocks[4:])]
    )


def body(state, star, flux, cluster, neighbour, orient, plane, thick,
         stiffness, trace_maps, lift_maps, rotations):
    stars = star.transpose(1, 2, 0, 3).reshape(Q * Q, 3, E).astype(F32)
    flux = flux.transpose(0, 2, 3, 1, 4).reshape(2 * Q * Q, 4, E)
    lift_maps = lift_maps.transpose(2, 0, 1)
    cluster = cluster.reshape(1, E)
    kept = [shape((3 * PAD, WIDE), BF16), shape((4 * AP, WIDE)), shape((Q, 40, E))]
    sends = [shape(dims) for dims in SENDS]
    split = shape((2 * Q * AP, ALL), BF16)
    products = [shape((3 * rows, 3 * reads), BF16) for rows, reads in STEPS]
    products.append(shape((4 * AP, 3 * PAD), BF16))
    own_outs = [kept[2], kept[1], shape((2 * Q * AP, ALL))]
    x_early, s_early, coarse, hot, marks, l_early, *rest = call(
        first_kernel,
        (state, stars, stiffness, trace_maps, plane, thick, neighbour, orient, cluster),
        kept + [shape((CP, ALL), BF16), shape((AP, E), jnp.int32), split]
        + products + sends,
        [PADDED, PADDED, X, Y],
        100_000_000, (4, 5),
    )
    steps, out_early = rest[:5], rest[5:]
    in_early = exchange(out_early)
    held, own, picked, solvers, same, volumes, lifts, turns = call(
        early_own_kernel,
        (state, x_early, s_early, l_early, stars, flux, marks, stiffness, lift_maps, rotations),
        own_outs + [
            shape((2 * Q * Q, 4, E)), shape((ALL, ALL), BF16), shape((120, 3 * PAD), BF16),
            shape((40, 12 * AP), BF16), shape((3 * AP, 3 * AP), BF16),
        ],
        [pltpu.VMEM((Q, 40, E), F32), Y], 200_000_000,
    )
    middle, x_late, s_late, l_late, *out_late = call(
        middle_kernel,
        (held, own, picked, coarse, hot, marks, stars, solvers, lifts, turns, *steps,
         *in_early),
        [kept[2], kept[0], kept[1], split] + sends,
        [PADDED, PADDED, X, Y, TURNED, SIDE, SIDE], 200_000_000,
    )
    in_late = exchange(out_late)
    held, own, picked = call(
        late_own_kernel, (middle, x_late, s_late, l_late, stars, solvers, volumes, same),
        own_outs, [Y], 200_000_000,
    )
    return call(
        last_kernel, (held, own, picked, hot, marks, solvers, lifts, turns, *in_late),
        shape((Q, B, E)), [TURNED, SIDE, SIDE], 100_000_000,
    )


def solution(mesh):
    both = ("dom", "ply")
    in_specs = (
        P(None, None, both),
        P(None, None, None, both),
        P(None, None, None, None, both),
        P(both),
        P(None, both),
        P(None, both),
        P(both, None),
        P(both, None),
        P(),
        P(),
        P(),
        P(),
    )
    return jax.shard_map(
        body, mesh=mesh, in_specs=in_specs, out_specs=P(None, None, both), check_vma=False
    )
```

```python
import jax
import jax.numpy as jnp
from jax import lax
from jax.experimental import pallas as pl
from jax.experimental.pallas import tpu as pltpu
from jax.sharding import PartitionSpec as P

F32, BF16 = jnp.float32, jnp.bfloat16
Q, B, A, ORDER = 9, 35, 15, 5
E = 128
PAD = 48
AP = 16
THICK, PLANE = 9, 16
SLOT, LAY = 8, 16
CUTS = 5 * SLOT + 2 * LAY
CP = 80
WIDE = Q * E
ALL = 4 * E

EARLY = [0.5 ** (k + 1) for k in range(ORDER)]
LATE = [1.0 - 0.5 ** (k + 1) for k in range(ORDER)]
FACT = [1.0, 2.0, 6.0, 24.0, 120.0]
STEPS = [(24, 48), (16, 48), (8, 32), (8, 16)]


def dot(a, b):
    return jnp.dot(a, b, preferred_element_type=F32)


def halves(x):
    top = x.astype(BF16)
    return top, (x - top.astype(F32)).astype(BF16)


def tripled(a):
    top = a.astype(BF16).astype(F32)
    return jnp.concatenate([top, top, a - top], axis=1).astype(BF16)


def padded(a, rows, cols):
    r, c = a.shape
    if c < cols:
        a = jnp.concatenate([a, jnp.zeros((r, cols - c), a.dtype)], axis=1)
    if r < rows:
        a = jnp.concatenate([a, jnp.zeros((rows - r, cols), a.dtype)], axis=0)
    return a


def lanes(p):
    return slice(p * E, (p + 1) * E)


def put_stack(ref, p, value, at=0, reach=PAD):
    top, rest = halves(value)
    for n, part in enumerate((top, rest, top)):
        ref[n * reach + at : n * reach + at + value.shape[0], lanes(p)] = part


def stiff_rows(stiffness):
    return [tripled(padded(stiffness[d][0:24], 24, PAD)).astype(F32) for d in range(3)]


def trace_rows(trace_maps):
    blocks = [tripled(padded(trace_maps[:, f, :], AP, PAD)).astype(F32) for f in range(4)]
    return jnp.concatenate(blocks, axis=0).astype(BF16)


def volume_rows(stiffness):
    blocks = [tripled(padded(stiffness[d].T, 40, PAD)).astype(F32) for d in range(3)]
    return jnp.concatenate(blocks, axis=0).astype(BF16)


def lift_rows(lift_maps):
    return tripled(jnp.concatenate([padded(lift_maps[:, f, :].T, 40, AP) for f in range(4)], axis=1))


def turn_rows(face_rotations):
    blocks = [tripled(padded(face_rotations[h], AP, AP)).astype(F32) for h in range(3)]
    return jnp.concatenate(blocks, axis=0)


def widen(source, target, blocks):
    for n in range(blocks):
        target[n] = source[n].astype(F32)


def star_apply(y, stars, rows):
    def one(p, total):
        total = list(total)
        at = pl.ds(pl.multiple_of(p * E, E), E)
        for d in range(3):
            value = y[d * rows : (d + 1) * rows, at]
            for q in range(Q):
                total[q] = total[q] + stars[q * Q + p, d : d + 1, :] * value
        return tuple(total)

    start = tuple(jnp.zeros((rows, E), F32) for _ in range(Q))
    return lax.fori_loop(0, Q, one, start, unroll=Q if rows < 40 else 3)


def taylor(first, steps, stars, x, y, add):
    values = [first[q] for q in range(Q)]
    for k, (rows, writes) in enumerate(STEPS):
        for p in range(Q):
            put_stack(x, p, padded(values[p], writes, E))
        y[0 : 3 * rows, :] = dot(steps[k][...], x[...])
        values = star_apply(y, stars, rows)
        for q in range(Q):
            add(k + 1, q, rows, values[q])


def far_steps(count):
    return (count - 3, count // 2)


def near_steps(count):
    return (count - 1, 3, 1)


def shared_faces(marks):
    dom, ply = lax.axis_index("dom"), lax.axis_index("ply")
    count = lax.axis_size("dom")
    odd, high = lax.rem(dom, 2), lax.rem(ply, 2)

    def column(row, start):
        dims = (SLOT, row.shape[1])
        sub = lax.broadcasted_iota(jnp.int32, dims, 0)
        lane = lax.broadcasted_iota(jnp.int32, dims, 1)
        picked = jnp.where(lane == sub + start, row.astype(F32), 0.0)
        return jnp.sum(picked, axis=1, keepdims=True)

    def plane_column(step):
        peer = lax.rem(dom + jnp.where(odd == 0, step, count - step), count)
        tile = E // SLOT
        return column(marks[pl.ds(PLANE + peer // tile, 1), :], lax.rem(peer, tile) * SLOT)

    def thick_columns(row):
        values = marks[pl.ds(THICK + row, 1), :]
        return [column(values, half) for half in (0, SLOT)]

    return (
        [plane_column(step) for step in far_steps(count)]
        + thick_columns(1 - high)
        + thick_columns(high)
        + [plane_column(step) for step in near_steps(count)]
    )


def pick_shared(marks, hot):
    columns = shared_faces(marks)
    columns.append(jnp.full((SLOT, 1), -1.0, F32))
    lane = lax.broadcasted_iota(jnp.int32, (AP, E), 1).astype(F32)
    for n in range(0, len(columns), 2):
        column = jnp.concatenate(columns[n : n + 2], axis=0)
        for f in range(4):
            hot[n * SLOT : (n + 2) * SLOT, lanes(f)] = jnp.where(
                column == lane + float(f * E), 1.0, 0.0
            ).astype(BF16)


def send_traces(s, hot, l, outs):
    split_traces(s, l)
    total = None
    for part in (1, 0):
        piece = lax.dot_general(
            hot[...],
            l[part * Q * AP : (part + 1) * Q * AP, :],
            (((1,), (1,)), ((), ())),
            preferred_element_type=F32,
        )
        total = piece if total is None else total + piece
    at = 0
    for out in outs[:-1]:
        out[...] = total[at : at + out.shape[0]]
        at += out.shape[0]
    outs[-1][...] = jnp.zeros_like(outs[-1])
    outs[-1][0:SLOT] = total[at : at + SLOT]


def split_traces(s, l):
    for q in range(Q):
        for f in range(4):
            top, rest = halves(s[f * AP : (f + 1) * AP, lanes(q)])
            l[q * AP : (q + 1) * AP, lanes(f)] = top
            l[Q * AP + q * AP : Q * AP + (q + 1) * AP, lanes(f)] = rest


def first_kernel(state, stars, stiffness, trace_maps, marks,
                 x_out, s_out, coarse, hot, l, step1, step2, step3, traces, *rest):
    sends, (first, early, x, y) = rest[:7], rest[7:]
    steps = (step1, step2, step3, step3)
    blocks = stiff_rows(stiffness)
    for step, (rows, _) in zip(steps, STEPS):
        step[...] = jnp.concatenate([block[0:rows] for block in blocks], axis=0).astype(BF16)
    traces[...] = trace_rows(trace_maps)
    pick_shared(marks, hot)
    first[...] = jnp.zeros_like(first)
    first[:, 0:B, :] = state[...]
    early[...] = first[...] * EARLY[0]
    coarse[...] = first[:, 0:40, :] * LATE[0]

    def add(k, q, rows, value):
        sign = -1.0 if k % 2 else 1.0
        early[q, 0:rows, :] = early[q, 0:rows, :] + value * (sign * EARLY[k] / FACT[k])
        coarse[q, 0:rows, :] = coarse[q, 0:rows, :] + value * (sign * LATE[k] / FACT[k])

    taylor(first, steps, stars, x, y, add)
    for p in range(Q):
        put_stack(x_out, p, early[p])
    s_out[...] = dot(traces[...], x_out[...])
    send_traces(s_out, hot, l, sends)


def put_near(near, picked):
    for q in range(Q):
        cols = slice(q * ALL, (q + 1) * ALL)
        near[0:AP, cols] = picked[q * AP : (q + 1) * AP].astype(BF16)
        near[AP : 2 * AP, cols] = picked[(Q + q) * AP : (Q + q + 1) * AP].astype(BF16)


def own_part(base, x, s, l, stars, solvers, volumes, same, held, own, near, y):
    put_near(near, dot(l[...], same[...]))
    y[...] = dot(volumes[...], x[...])
    sums = star_apply(y, stars, 40)
    for q in range(Q):
        held[q] = base(q) + sums[q]
    for f, rows, total in fluxes(solvers, 0, s, None):
        for q in range(Q):
            own[rows, lanes(q)] = total[q]


def fluxes(solvers, side, values, before):
    for f in range(4):
        rows = slice(f * AP, (f + 1) * AP)

        def face(p, total):
            total = list(total)
            at = pl.ds(pl.multiple_of(p * E, E), E)
            value = values[rows, at]
            for q in range(Q):
                total[q] = total[q] + solvers[(side * Q + q) * Q + p, f : f + 1, :] * value
            return tuple(total)

        start = [jnp.zeros((AP, E), F32) if before is None else before[rows, lanes(q)] for q in range(Q)]
        total = lax.fori_loop(0, Q, face, tuple(start), unroll=Q)
        yield f, rows, total


def early_own_kernel(state, x, s, l, stars, flux, marks, stiffness, lift_maps, rotations,
                     held, own, near, solvers, same, volumes, lifts, turns, padded_state, y):
    widen(flux, solvers, 2 * Q * Q)
    sub = lax.broadcasted_iota(jnp.int32, (ALL, E), 0)
    for f in range(4):
        same[:, lanes(f)] = jnp.where(sub == marks[f : f + 1, :], 1.0, 0.0).astype(BF16)
    volumes[...] = volume_rows(stiffness)
    lifts[...] = lift_rows(lift_maps)
    turns[...] = turn_rows(rotations).astype(BF16)
    padded_state[...] = jnp.zeros_like(padded_state)
    padded_state[:, 0:B, :] = state[...]
    own_part(lambda q: padded_state[q], x, s, l, stars, solvers, volumes, same, held, own, near, y)


def late_own_kernel(middle, x, s, l, stars, solvers, volumes, same, held, own, near, y):
    own_part(lambda q: middle[q], x, s, l, stars, solvers, volumes, same, held, own, near, y)


def finished(held, own, near, arrived, hot, marks, solvers, lifts, turns, o, g, y):
    landed = jnp.concatenate(
        [ref[...] for ref in arrived[:-1]]
        + [arrived[-1][0:SLOT], jnp.zeros((CP - CUTS, Q * AP), F32)],
        axis=0,
    )
    pieces = [
        lax.dot_general(piece, hot[...], (((0,), (0,)), ((), ())), preferred_element_type=F32)
        for piece in halves(landed)
    ]
    ways = [jnp.broadcast_to(marks[4 + f : 5 + f, :], (AP, E)) for f in range(4)]
    masks = [(way == 0, way == 1) for way in ways]
    for q in range(Q):
        cols = slice(q * ALL, (q + 1) * ALL)
        top = near[0:AP, cols] + pieces[0][q * AP : (q + 1) * AP].astype(BF16)
        rest = near[AP : 2 * AP, cols] + pieces[1][q * AP : (q + 1) * AP].astype(BF16)
        turned = dot(turns[...], jnp.concatenate([top, rest, top], axis=0))
        for f in range(4):
            first, second = masks[f]
            o[f * AP : (f + 1) * AP, lanes(q)] = jnp.where(
                first,
                turned[0:AP, lanes(f)],
                jnp.where(second, turned[AP : 2 * AP, lanes(f)], turned[2 * AP : 3 * AP, lanes(f)]),
            )
    for f, rows, total in fluxes(solvers, 1, o, own):
        for q in range(Q):
            put_stack(g, q, total[q], f * AP, 4 * AP)
    y[...] = dot(lifts[...], g[...])
    return [held[q] - y[:, lanes(q)] for q in range(Q)]


def middle_kernel(held, own, near, coarse, hot, marks, stars, solvers, lifts, turns,
                  step1, step2, step3, traces, *rest):
    arrived, (middle, x_out, s_out, l), sends = rest[:7], rest[7:11], rest[11:18]
    first, late, x, y, lifted, o, g = rest[18:]
    values = finished(
        held, own, near, arrived, hot, marks, solvers, lifts, turns, o, g, lifted
    )
    for q in range(Q):
        first[q] = padded(values[q], PAD, E)
        middle[q] = values[q]
        late[q] = first[q] * EARLY[0]

    def add(k, q, rows, value):
        sign = -1.0 if k % 2 else 1.0
        late[q, 0:rows, :] = late[q, 0:rows, :] + value * (sign * EARLY[k] / FACT[k])

    taylor(first, (step1, step2, step3, step3), stars, x, y, add)
    fine = marks[8:9, :] == 1
    for q in range(Q):
        late[q, 0:40, :] = jnp.where(fine, late[q, 0:40, :], coarse[q])
        put_stack(x_out, q, late[q])
    s_out[...] = dot(traces[...], x_out[...])
    send_traces(s_out, hot, l, sends)


def last_kernel(held, own, near, hot, marks, solvers, lifts, turns, *rest):
    arrived, out, (o, g, lifted) = rest[:7], rest[7], rest[8:]
    values = finished(
        held, own, near, arrived, hot, marks, solvers, lifts, turns, o, g, lifted
    )
    for q in range(Q):
        out[q] = values[q][0:B]


def shape(dims, kind=F32):
    return jax.ShapeDtypeStruct(dims, kind)


CORE_ROWS = 24
SENDS = (
    [(SLOT, Q * AP)] * 2 + [(LAY, Q * AP)] * 2 + [(SLOT, Q * AP)] * 2 + [(CORE_ROWS, Q * AP)]
)
PADDED = pltpu.VMEM((Q, PAD, E), F32)
X = pltpu.VMEM((3 * PAD, WIDE), BF16)
Y = pltpu.VMEM((120, WIDE), F32)
SIDE = pltpu.VMEM((4 * AP, WIDE), F32)
STACK = pltpu.VMEM((12 * AP, WIDE), BF16)
LIFTED = pltpu.VMEM((40, WIDE), F32)


def call(kernel, operands, outs, scratch, flops):
    vmem = pl.BlockSpec(memory_space=pltpu.VMEM)
    return pl.pallas_call(
        kernel,
        out_shape=outs,
        in_specs=[vmem] * len(operands),
        out_specs=jax.tree.map(lambda _: vmem, outs),
        scratch_shapes=scratch,
        compiler_params=pltpu.CompilerParams(vmem_limit_bytes=40 * 1024 * 1024),
        cost_estimate=pl.CostEstimate(flops=flops, bytes_accessed=2_000_000, transcendentals=0),
    )(*operands)


def exchange(blocks):
    count, layers = lax.axis_size("dom"), lax.axis_size("ply")

    def along_dom(step, block):
        if step % 2 == 0:
            pairs = [(i, (i + step) % count) for i in range(count)]
        else:
            pairs = []
            for even in range(0, count, 2):
                other = (even + step) % count
                pairs += [(even, other), (other, even)]
        return lax.ppermute(block, "dom", pairs)

    def along_ply(start, block):
        pairs = []
        for low in range(start, layers - 1, 2):
            pairs += [(low, low + 1), (low + 1, low)]
        return lax.ppermute(block, "ply", pairs)

    return (
        [along_dom(step, block) for step, block in zip(far_steps(count), blocks)]
        + [along_ply(start, block) for start, block in zip((0, 1), blocks[2:])]
        + [along_dom(step, block) for step, block in zip(near_steps(count), blocks[4:])]
    )


def body(state, star, flux, cluster, neighbour, orient, plane, thick,
         stiffness, trace_maps, lift_maps, rotations):
    stars = star.transpose(1, 2, 0, 3).reshape(Q * Q, 3, E).astype(F32)
    flux = flux.transpose(0, 2, 3, 1, 4).reshape(2 * Q * Q, 4, E)
    trace_maps = trace_maps.transpose(1, 0, 2)
    lift_maps = lift_maps.transpose(2, 0, 1)
    marks = jnp.concatenate(
        [
            neighbour,
            orient,
            cluster.reshape(1, E),
            jnp.pad(thick, ((0, 0), (0, E - LAY))),
            jnp.zeros((PLANE - THICK - 2, E), jnp.int32),
            plane.reshape(-1, E),
        ],
        axis=0,
    )
    kept = [shape((3 * PAD, WIDE), BF16), shape((4 * AP, WIDE)), shape((Q, 40, E))]
    sends = [shape(dims) for dims in SENDS]
    split = shape((2 * Q * AP, ALL), BF16)
    products = [shape((3 * rows, 3 * PAD), BF16) for rows, _ in STEPS[:3]]
    products.append(shape((4 * AP, 3 * PAD), BF16))
    own_outs = [kept[2], kept[1], shape((2 * AP, Q * ALL), BF16)]
    x_early, s_early, coarse, hot, l_early, *rest = call(
        first_kernel,
        (state, stars, stiffness, trace_maps, marks),
        kept + [shape((CP, ALL), BF16), split]
        + products + sends,
        [PADDED, PADDED, X, Y],
        100_000_000,
    )
    steps, out_early = rest[:4], rest[4:]
    in_early = exchange(out_early)
    held, own, near, solvers, same, volumes, lifts, turns = call(
        early_own_kernel,
        (state, x_early, s_early, l_early, stars, flux, marks, stiffness, lift_maps, rotations),
        own_outs + [
            shape((2 * Q * Q, 4, E)), shape((ALL, ALL), BF16), shape((120, 3 * PAD), BF16),
            shape((40, 12 * AP), BF16), shape((3 * AP, 3 * AP), BF16),
        ],
        [pltpu.VMEM((Q, 40, E), F32), Y], 200_000_000,
    )
    middle, x_late, s_late, l_late, *out_late = call(
        middle_kernel,
        (held, own, near, coarse, hot, marks, stars, solvers, lifts, turns, *steps,
         *in_early),
        [kept[2], kept[0], kept[1], split] + sends,
        [PADDED, PADDED, X, Y, LIFTED, SIDE, STACK], 200_000_000,
    )
    in_late = exchange(out_late)
    held, own, near = call(
        late_own_kernel, (middle, x_late, s_late, l_late, stars, solvers, volumes, same),
        own_outs, [Y], 200_000_000,
    )
    return call(
        last_kernel, (held, own, near, hot, marks, solvers, lifts, turns, *in_late),
        shape((Q, B, E)), [SIDE, STACK, LIFTED], 100_000_000,
    )


def solution(mesh):
    both = ("dom", "ply")
    in_specs = (
        P(None, None, both),
        P(None, None, None, both),
        P(None, None, None, None, both),
        P(both),
        P(None, both),
        P(None, both),
        P(both, None),
        P(both, None),
        P(),
        P(),
        P(),
        P(),
    )
    return jax.shard_map(
        body, mesh=mesh, in_specs=in_specs, out_specs=P(None, None, both), check_vma=False
    )
```

```python
import jax
import jax.numpy as jnp
from jax import lax
from jax.experimental import pallas as pl
from jax.experimental.pallas import tpu as pltpu
from jax.sharding import PartitionSpec as P

F32, BF16 = jnp.float32, jnp.bfloat16
Q, B, A, ORDER = 9, 35, 15, 5
E = 128
PAD = 48
AP = 16
THICK, PLANE = 9, 16
SLOT, LAY = 8, 16
CUTS = 5 * SLOT + 2 * LAY
CP = 80
WIDE = Q * E
ALL = 4 * E

EARLY = [0.5 ** (k + 1) for k in range(ORDER)]
LATE = [1.0 - 0.5 ** (k + 1) for k in range(ORDER)]
FACT = [1.0, 2.0, 6.0, 24.0, 120.0]
STEPS = [(24, 48), (16, 48), (8, 32), (8, 16)]


def dot(a, b):
    return jnp.dot(a, b, preferred_element_type=F32)


def halves(x):
    top = x.astype(BF16)
    return top, (x - top.astype(F32)).astype(BF16)


def tripled(a):
    top = a.astype(BF16).astype(F32)
    return jnp.concatenate([top, top, a - top], axis=1).astype(BF16)


def padded(a, rows, cols):
    r, c = a.shape
    if c < cols:
        a = jnp.concatenate([a, jnp.zeros((r, cols - c), a.dtype)], axis=1)
    if r < rows:
        a = jnp.concatenate([a, jnp.zeros((rows - r, cols), a.dtype)], axis=0)
    return a


def lanes(p):
    return slice(p * E, (p + 1) * E)


def put_stack(ref, p, value, at=0, reach=PAD):
    top, rest = halves(value)
    for n, part in enumerate((top, rest, top)):
        ref[n * reach + at : n * reach + at + value.shape[0], lanes(p)] = part


def stiff_rows(stiffness):
    return [tripled(padded(stiffness[d][0:24], 24, PAD)).astype(F32) for d in range(3)]


def trace_rows(trace_maps):
    blocks = [tripled(padded(trace_maps[:, f, :], AP, PAD)).astype(F32) for f in range(4)]
    return jnp.concatenate(blocks, axis=0).astype(BF16)


def volume_rows(stiffness):
    blocks = [tripled(padded(stiffness[d].T, 40, PAD)).astype(F32) for d in range(3)]
    return jnp.concatenate(blocks, axis=0).astype(BF16)


def lift_rows(lift_maps):
    return tripled(jnp.concatenate([padded(lift_maps[:, f, :].T, 40, AP) for f in range(4)], axis=1))


def turn_rows(face_rotations):
    blocks = [tripled(padded(face_rotations[h], AP, AP)).astype(F32) for h in range(3)]
    return jnp.concatenate(blocks, axis=0)


def widen(source, target, blocks):
    for n in range(blocks):
        target[n] = source[n].astype(F32)


def star_apply(y, stars, rows):
    def one(p, total):
        total = list(total)
        at = pl.ds(pl.multiple_of(p * E, E), E)
        for d in range(3):
            value = y[d * rows : (d + 1) * rows, at]
            for q in range(Q):
                total[q] = total[q] + stars[q * Q + p, d : d + 1, :] * value
        return tuple(total)

    start = tuple(jnp.zeros((rows, E), F32) for _ in range(Q))
    return lax.fori_loop(0, Q, one, start, unroll=Q if rows < 40 else 3)


def taylor(first, steps, stars, x, y, add):
    values = [first[q] for q in range(Q)]
    for k, (rows, writes) in enumerate(STEPS):
        for p in range(Q):
            put_stack(x, p, padded(values[p], writes, E))
        y[0 : 3 * rows, :] = dot(steps[k][...], x[...])
        values = star_apply(y, stars, rows)
        for q in range(Q):
            add(k + 1, q, rows, values[q])


def far_steps(count):
    return (count - 1, 3, count - 3, count // 2)


def near_steps(count):
    return (1,)


def shared_faces(marks):
    dom, ply = lax.axis_index("dom"), lax.axis_index("ply")
    count = lax.axis_size("dom")
    odd, high = lax.rem(dom, 2), lax.rem(ply, 2)

    def column(row, start):
        dims = (SLOT, row.shape[1])
        sub = lax.broadcasted_iota(jnp.int32, dims, 0)
        lane = lax.broadcasted_iota(jnp.int32, dims, 1)
        picked = jnp.where(lane == sub + start, row.astype(F32), 0.0)
        return jnp.sum(picked, axis=1, keepdims=True)

    def plane_column(step):
        peer = lax.rem(dom + jnp.where(odd == 0, step, count - step), count)
        tile = E // SLOT
        return column(marks[pl.ds(PLANE + peer // tile, 1), :], lax.rem(peer, tile) * SLOT)

    def thick_columns(row):
        values = marks[pl.ds(THICK + row, 1), :]
        return [column(values, half) for half in (0, SLOT)]

    return (
        [plane_column(step) for step in far_steps(count)]
        + thick_columns(1 - high)
        + thick_columns(high)
        + [plane_column(step) for step in near_steps(count)]
    )


def pick_shared(marks, hot):
    columns = shared_faces(marks)
    columns.append(jnp.full((SLOT, 1), -1.0, F32))
    lane = lax.broadcasted_iota(jnp.int32, (AP, E), 1).astype(F32)
    for n in range(0, len(columns), 2):
        column = jnp.concatenate(columns[n : n + 2], axis=0)
        for f in range(4):
            hot[n * SLOT : (n + 2) * SLOT, lanes(f)] = jnp.where(
                column == lane + float(f * E), 1.0, 0.0
            ).astype(BF16)


def send_traces(s, hot, l, outs):
    split_traces(s, l)
    total = None
    for part in (1, 0):
        piece = lax.dot_general(
            hot[...],
            l[part * Q * AP : (part + 1) * Q * AP, :],
            (((1,), (1,)), ((), ())),
            preferred_element_type=F32,
        )
        total = piece if total is None else total + piece
    at = 0
    for out in outs[:-1]:
        out[...] = total[at : at + out.shape[0]]
        at += out.shape[0]
    outs[-1][...] = jnp.zeros_like(outs[-1])
    outs[-1][0:SLOT] = total[at : at + SLOT]


def split_traces(s, l):
    for q in range(Q):
        for f in range(4):
            top, rest = halves(s[f * AP : (f + 1) * AP, lanes(q)])
            l[q * AP : (q + 1) * AP, lanes(f)] = top
            l[Q * AP + q * AP : Q * AP + (q + 1) * AP, lanes(f)] = rest


def first_kernel(state, stars, stiffness, trace_maps, marks,
                 x_out, s_out, coarse, hot, l, step1, step2, step3, traces, *rest):
    sends, (first, early, x, y) = rest[:7], rest[7:]
    steps = (step1, step2, step3, step3)
    blocks = stiff_rows(stiffness)
    for step, (rows, _) in zip(steps, STEPS):
        step[...] = jnp.concatenate([block[0:rows] for block in blocks], axis=0).astype(BF16)
    traces[...] = trace_rows(trace_maps)
    pick_shared(marks, hot)
    first[...] = jnp.zeros_like(first)
    first[:, 0:B, :] = state[...]
    early[...] = first[...] * EARLY[0]
    coarse[...] = first[:, 0:40, :] * LATE[0]

    def add(k, q, rows, value):
        sign = -1.0 if k % 2 else 1.0
        early[q, 0:rows, :] = early[q, 0:rows, :] + value * (sign * EARLY[k] / FACT[k])
        coarse[q, 0:rows, :] = coarse[q, 0:rows, :] + value * (sign * LATE[k] / FACT[k])

    taylor(first, steps, stars, x, y, add)
    for p in range(Q):
        put_stack(x_out, p, early[p])
    s_out[...] = dot(traces[...], x_out[...])
    send_traces(s_out, hot, l, sends)


def put_near(near, picked):
    for q in range(Q):
        cols = slice(q * ALL, (q + 1) * ALL)
        near[0:AP, cols] = picked[q * AP : (q + 1) * AP].astype(BF16)
        near[AP : 2 * AP, cols] = picked[(Q + q) * AP : (Q + q + 1) * AP].astype(BF16)


def own_part(base, x, s, l, stars, solvers, volumes, same, held, own, near, y):
    put_near(near, dot(l[...], same[...]))
    y[...] = dot(volumes[...], x[...])
    sums = star_apply(y, stars, 40)
    for q in range(Q):
        held[q] = base(q) + sums[q]
    for f, rows, total in fluxes(solvers, 0, s, None):
        for q in range(Q):
            own[rows, lanes(q)] = total[q]


def fluxes(solvers, side, values, before):
    for f in range(4):
        rows = slice(f * AP, (f + 1) * AP)

        def face(p, total):
            total = list(total)
            at = pl.ds(pl.multiple_of(p * E, E), E)
            value = values[rows, at]
            for q in range(Q):
                total[q] = total[q] + solvers[(side * Q + q) * Q + p, f : f + 1, :] * value
            return tuple(total)

        start = [jnp.zeros((AP, E), F32) if before is None else before[rows, lanes(q)] for q in range(Q)]
        total = lax.fori_loop(0, Q, face, tuple(start), unroll=Q)
        yield f, rows, total


def early_own_kernel(state, x, s, l, stars, flux, marks, stiffness, lift_maps, rotations,
                     held, own, near, solvers, same, volumes, lifts, turns, padded_state, y):
    widen(flux, solvers, 2 * Q * Q)
    sub = lax.broadcasted_iota(jnp.int32, (ALL, E), 0)
    for f in range(4):
        same[:, lanes(f)] = jnp.where(sub == marks[f : f + 1, :], 1.0, 0.0).astype(BF16)
    volumes[...] = volume_rows(stiffness)
    lifts[...] = lift_rows(lift_maps)
    turns[...] = turn_rows(rotations).astype(BF16)
    padded_state[...] = jnp.zeros_like(padded_state)
    padded_state[:, 0:B, :] = state[...]
    own_part(lambda q: padded_state[q], x, s, l, stars, solvers, volumes, same, held, own, near, y)


def late_own_kernel(middle, x, s, l, stars, solvers, volumes, same, held, own, near, y):
    own_part(lambda q: middle[q], x, s, l, stars, solvers, volumes, same, held, own, near, y)


def finished(held, own, near, arrived, hot, marks, solvers, lifts, turns, o, g):
    landed = jnp.concatenate(
        [ref[...] for ref in arrived[:-1]]
        + [arrived[-1][0:SLOT], jnp.zeros((CP - CUTS, Q * AP), F32)],
        axis=0,
    )
    pieces = [
        lax.dot_general(piece, hot[...], (((0,), (0,)), ((), ())), preferred_element_type=F32)
        for piece in halves(landed)
    ]
    ways = [jnp.broadcast_to(marks[4 + f : 5 + f, :], (AP, E)) for f in range(4)]
    masks = [(way == 0, way == 1) for way in ways]
    for q in range(Q):
        cols = slice(q * ALL, (q + 1) * ALL)
        top = near[0:AP, cols] + pieces[0][q * AP : (q + 1) * AP].astype(BF16)
        rest = near[AP : 2 * AP, cols] + pieces[1][q * AP : (q + 1) * AP].astype(BF16)
        turned = dot(turns[...], jnp.concatenate([top, rest, top], axis=0))
        for f in range(4):
            first, second = masks[f]
            o[f * AP : (f + 1) * AP, lanes(q)] = jnp.where(
                first,
                turned[0:AP, lanes(f)],
                jnp.where(second, turned[AP : 2 * AP, lanes(f)], turned[2 * AP : 3 * AP, lanes(f)]),
            )
    for f, rows, total in fluxes(solvers, 1, o, own):
        for q in range(Q):
            put_stack(g, q, total[q], f * AP, 4 * AP)
    results = []
    for q in range(0, Q, 2):
        group = range(q, min(q + 2, Q))
        lifted = dot(lifts[...], g[:, q * E : (group[-1] + 1) * E])
        results += [held[n] - lifted[:, lanes(n - q)] for n in group]
    return results


def middle_kernel(held, own, near, coarse, hot, marks, stars, solvers, lifts, turns,
                  step1, step2, step3, traces, *rest):
    arrived, (middle, x_out, s_out, l), sends = rest[:7], rest[7:11], rest[11:18]
    first, late, x, y, o, g = rest[18:]
    values = finished(
        held, own, near, arrived, hot, marks, solvers, lifts, turns, o, g
    )
    for q in range(Q):
        first[q] = padded(values[q], PAD, E)
        middle[q] = values[q]
        late[q] = first[q] * EARLY[0]

    def add(k, q, rows, value):
        sign = -1.0 if k % 2 else 1.0
        late[q, 0:rows, :] = late[q, 0:rows, :] + value * (sign * EARLY[k] / FACT[k])

    taylor(first, (step1, step2, step3, step3), stars, x, y, add)
    fine = marks[8:9, :] == 1
    for q in range(Q):
        late[q, 0:40, :] = jnp.where(fine, late[q, 0:40, :], coarse[q])
        put_stack(x_out, q, late[q])
    s_out[...] = dot(traces[...], x_out[...])
    send_traces(s_out, hot, l, sends)


def last_kernel(held, own, near, hot, marks, solvers, lifts, turns, *rest):
    arrived, out, (o, g) = rest[:7], rest[7], rest[8:]
    values = finished(
        held, own, near, arrived, hot, marks, solvers, lifts, turns, o, g
    )
    for q in range(Q):
        out[q] = values[q][0:B]


def shape(dims, kind=F32):
    return jax.ShapeDtypeStruct(dims, kind)


CORE_ROWS = 24
SENDS = (
    [(SLOT, Q * AP)] * 4 + [(LAY, Q * AP)] * 2 + [(CORE_ROWS, Q * AP)]
)
PADDED = pltpu.VMEM((Q, PAD, E), F32)
X = pltpu.VMEM((3 * PAD, WIDE), BF16)
Y = pltpu.VMEM((120, WIDE), F32)
SIDE = pltpu.VMEM((4 * AP, WIDE), F32)
STACK = pltpu.VMEM((12 * AP, WIDE), BF16)


def call(kernel, operands, outs, scratch, flops):
    vmem = pl.BlockSpec(memory_space=pltpu.VMEM)
    return pl.pallas_call(
        kernel,
        out_shape=outs,
        in_specs=[vmem] * len(operands),
        out_specs=jax.tree.map(lambda _: vmem, outs),
        scratch_shapes=scratch,
        compiler_params=pltpu.CompilerParams(vmem_limit_bytes=40 * 1024 * 1024),
        cost_estimate=pl.CostEstimate(flops=flops, bytes_accessed=2_000_000, transcendentals=0),
    )(*operands)


def exchange(blocks):
    count, layers = lax.axis_size("dom"), lax.axis_size("ply")

    def along_dom(step, block):
        if step % 2 == 0:
            pairs = [(i, (i + step) % count) for i in range(count)]
        else:
            pairs = []
            for even in range(0, count, 2):
                other = (even + step) % count
                pairs += [(even, other), (other, even)]
        return lax.ppermute(block, "dom", pairs)

    def along_ply(start, block):
        pairs = []
        for low in range(start, layers - 1, 2):
            pairs += [(low, low + 1), (low + 1, low)]
        return lax.ppermute(block, "ply", pairs)

    return (
        [along_dom(step, block) for step, block in zip(far_steps(count), blocks)]
        + [along_ply(start, block) for start, block in zip((0, 1), blocks[4:])]
        + [along_dom(step, block) for step, block in zip(near_steps(count), blocks[6:])]
    )


def body(state, star, flux, cluster, neighbour, orient, plane, thick,
         stiffness, trace_maps, lift_maps, rotations):
    stars = star.transpose(1, 2, 0, 3).reshape(Q * Q, 3, E).astype(F32)
    flux = flux.transpose(0, 2, 3, 1, 4).reshape(2 * Q * Q, 4, E)
    trace_maps = trace_maps.transpose(1, 0, 2)
    lift_maps = lift_maps.transpose(2, 0, 1)
    marks = jnp.concatenate(
        [
            neighbour,
            orient,
            cluster.reshape(1, E),
            jnp.pad(thick, ((0, 0), (0, E - LAY))),
            jnp.zeros((PLANE - THICK - 2, E), jnp.int32),
            plane.reshape(-1, E),
        ],
        axis=0,
    )
    kept = [shape((3 * PAD, WIDE), BF16), shape((4 * AP, WIDE)), shape((Q, 40, E))]
    sends = [shape(dims) for dims in SENDS]
    split = shape((2 * Q * AP, ALL), BF16)
    products = [shape((3 * rows, 3 * PAD), BF16) for rows, _ in STEPS[:3]]
    products.append(shape((4 * AP, 3 * PAD), BF16))
    own_outs = [kept[2], kept[1], shape((2 * AP, Q * ALL), BF16)]
    x_early, s_early, coarse, hot, l_early, *rest = call(
        first_kernel,
        (state, stars, stiffness, trace_maps, marks),
        kept + [shape((CP, ALL), BF16), split]
        + products + sends,
        [PADDED, PADDED, X, Y],
        100_000_000,
    )
    steps, out_early = rest[:4], rest[4:]
    in_early = exchange(out_early)
    held, own, near, solvers, same, volumes, lifts, turns = call(
        early_own_kernel,
        (state, x_early, s_early, l_early, stars, flux, marks, stiffness, lift_maps, rotations),
        own_outs + [
            shape((2 * Q * Q, 4, E)), shape((ALL, ALL), BF16), shape((120, 3 * PAD), BF16),
            shape((40, 12 * AP), BF16), shape((3 * AP, 3 * AP), BF16),
        ],
        [pltpu.VMEM((Q, 40, E), F32), Y], 200_000_000,
    )
    middle, x_late, s_late, l_late, *out_late = call(
        middle_kernel,
        (held, own, near, coarse, hot, marks, stars, solvers, lifts, turns, *steps,
         *in_early),
        [kept[2], kept[0], kept[1], split] + sends,
        [PADDED, PADDED, X, Y, SIDE, STACK], 200_000_000,
    )
    in_late = exchange(out_late)
    held, own, near = call(
        late_own_kernel, (middle, x_late, s_late, l_late, stars, solvers, volumes, same),
        own_outs, [Y], 200_000_000,
    )
    return call(
        last_kernel, (held, own, near, hot, marks, solvers, lifts, turns, *in_late),
        shape((Q, B, E)), [SIDE, STACK], 100_000_000,
    )


def solution(mesh):
    both = ("dom", "ply")
    in_specs = (
        P(None, None, both),
        P(None, None, None, both),
        P(None, None, None, None, both),
        P(both),
        P(None, both),
        P(None, both),
        P(both, None),
        P(both, None),
        P(),
        P(),
        P(),
        P(),
    )
    return jax.shard_map(
        body, mesh=mesh, in_specs=in_specs, out_specs=P(None, None, both), check_vma=False
    )
```

```python
import jax
import jax.numpy as jnp
from jax import lax
from jax.experimental import pallas as pl
from jax.experimental.pallas import tpu as pltpu
from jax.sharding import PartitionSpec as P

F32, BF16 = jnp.float32, jnp.bfloat16
Q, B, A, ORDER = 9, 35, 15, 5
E = 128
PAD = 48
AP = 16
THICK, PLANE = 9, 16
SLOT, LAY = 8, 16
CUTS = 5 * SLOT + 2 * LAY
CP = 80
WIDE = Q * E
ALL = 4 * E

EARLY = [0.5 ** (k + 1) for k in range(ORDER)]
LATE = [1.0 - 0.5 ** (k + 1) for k in range(ORDER)]
FACT = [1.0, 2.0, 6.0, 24.0, 120.0]
STEPS = [(24, 48), (16, 48), (8, 32), (8, 16)]


def dot(a, b):
    return jnp.dot(a, b, preferred_element_type=F32)


def halves(x):
    top = x.astype(BF16)
    return top, (x - top.astype(F32)).astype(BF16)


def tripled(a):
    top = a.astype(BF16).astype(F32)
    return jnp.concatenate([top, top, a - top], axis=1).astype(BF16)


def padded(a, rows, cols):
    r, c = a.shape
    if c < cols:
        a = jnp.concatenate([a, jnp.zeros((r, cols - c), a.dtype)], axis=1)
    if r < rows:
        a = jnp.concatenate([a, jnp.zeros((rows - r, cols), a.dtype)], axis=0)
    return a


def lanes(p):
    return slice(p * E, (p + 1) * E)


def put_stack(ref, p, value, at=0, reach=PAD):
    top, rest = halves(value)
    for n, part in enumerate((top, rest, top)):
        ref[n * reach + at : n * reach + at + value.shape[0], lanes(p)] = part


def stiff_rows(stiffness):
    return [tripled(padded(stiffness[d][0:24], 24, PAD)).astype(F32) for d in range(3)]


def trace_rows(trace_maps):
    blocks = [tripled(padded(trace_maps[:, f, :], AP, PAD)).astype(F32) for f in range(4)]
    return jnp.concatenate(blocks, axis=0).astype(BF16)


def volume_rows(stiffness):
    blocks = [tripled(padded(stiffness[d].T, 40, PAD)).astype(F32) for d in range(3)]
    return jnp.concatenate(blocks, axis=0).astype(BF16)


def lift_rows(lift_maps):
    return tripled(jnp.concatenate([padded(lift_maps[:, f, :].T, 40, AP) for f in range(4)], axis=1))


def turn_rows(face_rotations):
    blocks = [tripled(padded(face_rotations[h], AP, AP)).astype(F32) for h in range(3)]
    return jnp.concatenate(blocks, axis=0)


def widen(source, target, blocks):
    for n in range(blocks):
        target[n] = source[n].astype(F32)


def star_apply(y, stars, rows):
    def one(p, total):
        total = list(total)
        at = pl.ds(pl.multiple_of(p * E, E), E)
        for d in range(3):
            value = y[d * rows : (d + 1) * rows, at]
            for q in range(Q):
                total[q] = total[q] + stars[q * Q + p, d : d + 1, :] * value
        return tuple(total)

    start = tuple(jnp.zeros((rows, E), F32) for _ in range(Q))
    return lax.fori_loop(0, Q, one, start, unroll=Q if rows < 40 else 3)


def taylor(first, steps, stars, x, y, add):
    values = [first[q] for q in range(Q)]
    for k, (rows, writes) in enumerate(STEPS):
        for p in range(Q):
            put_stack(x, p, padded(values[p], writes, E))
        y[0 : 3 * rows, :] = dot(steps[k][...], x[...])
        values = star_apply(y, stars, rows)
        for q in range(Q):
            add(k + 1, q, rows, values[q])


def far_steps(count):
    return (count - 1, 3, count - 3, count // 2)


def near_steps(count):
    return (1,)


def shared_faces(marks):
    dom, ply = lax.axis_index("dom"), lax.axis_index("ply")
    count = lax.axis_size("dom")
    odd, high = lax.rem(dom, 2), lax.rem(ply, 2)

    def column(row, start):
        dims = (SLOT, row.shape[1])
        sub = lax.broadcasted_iota(jnp.int32, dims, 0)
        lane = lax.broadcasted_iota(jnp.int32, dims, 1)
        picked = jnp.where(lane == sub + start, row.astype(F32), 0.0)
        return jnp.sum(picked, axis=1, keepdims=True)

    def plane_column(step):
        peer = lax.rem(dom + jnp.where(odd == 0, step, count - step), count)
        tile = E // SLOT
        return column(marks[pl.ds(PLANE + peer // tile, 1), :], lax.rem(peer, tile) * SLOT)

    def thick_columns(row):
        values = marks[pl.ds(THICK + row, 1), :]
        return [column(values, half) for half in (0, SLOT)]

    return (
        [plane_column(step) for step in far_steps(count)]
        + thick_columns(1 - high)
        + thick_columns(high)
        + [plane_column(step) for step in near_steps(count)]
    )


def pick_shared(marks, hot):
    columns = shared_faces(marks)
    columns.append(jnp.full((SLOT, 1), -1.0, F32))
    lane = lax.broadcasted_iota(jnp.int32, (AP, E), 1).astype(F32)
    for n in range(0, len(columns), 2):
        column = jnp.concatenate(columns[n : n + 2], axis=0)
        for f in range(4):
            hot[n * SLOT : (n + 2) * SLOT, lanes(f)] = jnp.where(
                column == lane + float(f * E), 1.0, 0.0
            ).astype(BF16)


def send_traces(s, hot, l, outs):
    split_traces(s, l)
    total = None
    for part in (1, 0):
        piece = lax.dot_general(
            hot[...],
            l[part * Q * AP : (part + 1) * Q * AP, :],
            (((1,), (1,)), ((), ())),
            preferred_element_type=F32,
        )
        total = piece if total is None else total + piece
    at = 0
    for out in outs[:-1]:
        out[...] = total[at : at + out.shape[0]]
        at += out.shape[0]
    outs[-1][...] = jnp.zeros_like(outs[-1])
    outs[-1][0:SLOT] = total[at : at + SLOT]


def split_traces(s, l):
    for q in range(Q):
        for f in range(4):
            top, rest = halves(s[f * AP : (f + 1) * AP, lanes(q)])
            l[q * AP : (q + 1) * AP, lanes(f)] = top
            l[Q * AP + q * AP : Q * AP + (q + 1) * AP, lanes(f)] = rest


def first_kernel(state, stars, stiffness, x_out, coarse, step1, step2, step3, first, early, x, y):
    steps = (step1, step2, step3, step3)
    blocks = stiff_rows(stiffness)
    for step, (rows, _) in zip(steps, STEPS):
        step[...] = jnp.concatenate([block[0:rows] for block in blocks], axis=0).astype(BF16)
    first[...] = jnp.zeros_like(first)
    first[:, 0:B, :] = state[...]
    early[...] = first[...] * EARLY[0]
    coarse[...] = first[:, 0:40, :] * LATE[0]

    def add(k, q, rows, value):
        sign = -1.0 if k % 2 else 1.0
        early[q, 0:rows, :] = early[q, 0:rows, :] + value * (sign * EARLY[k] / FACT[k])
        coarse[q, 0:rows, :] = coarse[q, 0:rows, :] + value * (sign * LATE[k] / FACT[k])

    taylor(first, steps, stars, x, y, add)
    for p in range(Q):
        put_stack(x_out, p, early[p])


def first_send_kernel(x, trace_maps, marks, s_out, l, hot, traces, *sends):
    pick_shared(marks, hot)
    traces[...] = trace_rows(trace_maps)
    s_out[...] = dot(traces[...], x[...])
    send_traces(s_out, hot, l, sends)


def put_near(near, picked):
    for q in range(Q):
        cols = slice(q * ALL, (q + 1) * ALL)
        near[0:AP, cols] = picked[q * AP : (q + 1) * AP].astype(BF16)
        near[AP : 2 * AP, cols] = picked[(Q + q) * AP : (Q + q + 1) * AP].astype(BF16)


def own_part(base, x, s, l, stars, solvers, volumes, same, held, own, near, y):
    put_near(near, dot(l[...], same[...]))
    y[...] = dot(volumes[...], x[...])
    sums = star_apply(y, stars, 40)
    for q in range(Q):
        held[q] = base(q) + sums[q]
    for f, rows, total in fluxes(solvers, 0, s, None):
        for q in range(Q):
            own[rows, lanes(q)] = total[q]


def fluxes(solvers, side, values, before):
    for f in range(4):
        rows = slice(f * AP, (f + 1) * AP)

        def face(p, total):
            total = list(total)
            at = pl.ds(pl.multiple_of(p * E, E), E)
            value = values[rows, at]
            for q in range(Q):
                total[q] = total[q] + solvers[(side * Q + q) * Q + p, f : f + 1, :] * value
            return tuple(total)

        start = [jnp.zeros((AP, E), F32) if before is None else before[rows, lanes(q)] for q in range(Q)]
        total = lax.fori_loop(0, Q, face, tuple(start), unroll=Q)
        yield f, rows, total


def early_own_kernel(state, x, s, l, stars, flux, marks, stiffness, lift_maps, rotations,
                     held, own, near, solvers, same, volumes, lifts, turns, padded_state, y):
    widen(flux, solvers, 2 * Q * Q)
    sub = lax.broadcasted_iota(jnp.int32, (ALL, E), 0)
    for f in range(4):
        same[:, lanes(f)] = jnp.where(sub == marks[f : f + 1, :], 1.0, 0.0).astype(BF16)
    volumes[...] = volume_rows(stiffness)
    lifts[...] = lift_rows(lift_maps)
    turns[...] = turn_rows(rotations).astype(BF16)
    padded_state[...] = jnp.zeros_like(padded_state)
    padded_state[:, 0:B, :] = state[...]
    own_part(lambda q: padded_state[q], x, s, l, stars, solvers, volumes, same, held, own, near, y)


def late_own_kernel(middle, x, s, l, stars, solvers, volumes, same, held, own, near, y):
    own_part(lambda q: middle[q], x, s, l, stars, solvers, volumes, same, held, own, near, y)


def finished(held, own, near, arrived, hot, marks, solvers, lifts, turns, o, g):
    landed = jnp.concatenate(
        [ref[...] for ref in arrived[:-1]]
        + [arrived[-1][0:SLOT], jnp.zeros((CP - CUTS, Q * AP), F32)],
        axis=0,
    )
    pieces = [
        lax.dot_general(piece, hot[...], (((0,), (0,)), ((), ())), preferred_element_type=F32)
        for piece in halves(landed)
    ]
    ways = [jnp.broadcast_to(marks[4 + f : 5 + f, :], (AP, E)) for f in range(4)]
    masks = [(way == 0, way == 1) for way in ways]
    for q in range(Q):
        cols = slice(q * ALL, (q + 1) * ALL)
        top = near[0:AP, cols] + pieces[0][q * AP : (q + 1) * AP].astype(BF16)
        rest = near[AP : 2 * AP, cols] + pieces[1][q * AP : (q + 1) * AP].astype(BF16)
        turned = dot(turns[...], jnp.concatenate([top, rest, top], axis=0))
        for f in range(4):
            first, second = masks[f]
            o[f * AP : (f + 1) * AP, lanes(q)] = jnp.where(
                first,
                turned[0:AP, lanes(f)],
                jnp.where(second, turned[AP : 2 * AP, lanes(f)], turned[2 * AP : 3 * AP, lanes(f)]),
            )
    for f, rows, total in fluxes(solvers, 1, o, own):
        for q in range(Q):
            put_stack(g, q, total[q], f * AP, 4 * AP)
    results = []
    for q in range(0, Q, 2):
        group = range(q, min(q + 2, Q))
        lifted = dot(lifts[...], g[:, q * E : (group[-1] + 1) * E])
        results += [held[n] - lifted[:, lanes(n - q)] for n in group]
    return results


def middle_kernel(held, own, near, coarse, hot, marks, stars, solvers, lifts, turns,
                  step1, step2, step3, traces, *rest):
    arrived, (middle, x_out, s_out, l), sends = rest[:7], rest[7:11], rest[11:18]
    first, late, x, y, o, g = rest[18:]
    values = finished(
        held, own, near, arrived, hot, marks, solvers, lifts, turns, o, g
    )
    for q in range(Q):
        first[q] = padded(values[q], PAD, E)
        middle[q] = values[q]
        late[q] = first[q] * EARLY[0]

    def add(k, q, rows, value):
        sign = -1.0 if k % 2 else 1.0
        late[q, 0:rows, :] = late[q, 0:rows, :] + value * (sign * EARLY[k] / FACT[k])

    taylor(first, (step1, step2, step3, step3), stars, x, y, add)
    fine = marks[8:9, :] == 1
    for q in range(Q):
        late[q, 0:40, :] = jnp.where(fine, late[q, 0:40, :], coarse[q])
        put_stack(x_out, q, late[q])
    s_out[...] = dot(traces[...], x_out[...])
    send_traces(s_out, hot, l, sends)


def last_kernel(held, own, near, hot, marks, solvers, lifts, turns, *rest):
    arrived, out, (o, g) = rest[:7], rest[7], rest[8:]
    values = finished(
        held, own, near, arrived, hot, marks, solvers, lifts, turns, o, g
    )
    for q in range(Q):
        out[q] = values[q][0:B]


def shape(dims, kind=F32):
    return jax.ShapeDtypeStruct(dims, kind)


CORE_ROWS = 24
SENDS = (
    [(SLOT, Q * AP)] * 4 + [(LAY, Q * AP)] * 2 + [(CORE_ROWS, Q * AP)]
)
PADDED = pltpu.VMEM((Q, PAD, E), F32)
X = pltpu.VMEM((3 * PAD, WIDE), BF16)
Y = pltpu.VMEM((120, WIDE), F32)
SIDE = pltpu.VMEM((4 * AP, WIDE), F32)
STACK = pltpu.VMEM((12 * AP, WIDE), BF16)


def call(kernel, operands, outs, scratch, flops):
    vmem = pl.BlockSpec(memory_space=pltpu.VMEM)
    return pl.pallas_call(
        kernel,
        out_shape=outs,
        in_specs=[vmem] * len(operands),
        out_specs=jax.tree.map(lambda _: vmem, outs),
        scratch_shapes=scratch,
        compiler_params=pltpu.CompilerParams(vmem_limit_bytes=40 * 1024 * 1024),
        cost_estimate=pl.CostEstimate(flops=flops, bytes_accessed=2_000_000, transcendentals=0),
    )(*operands)


def exchange(blocks):
    count, layers = lax.axis_size("dom"), lax.axis_size("ply")

    def along_dom(step, block):
        if step % 2 == 0:
            pairs = [(i, (i + step) % count) for i in range(count)]
        else:
            pairs = []
            for even in range(0, count, 2):
                other = (even + step) % count
                pairs += [(even, other), (other, even)]
        return lax.ppermute(block, "dom", pairs)

    def along_ply(start, block):
        pairs = []
        for low in range(start, layers - 1, 2):
            pairs += [(low, low + 1), (low + 1, low)]
        return lax.ppermute(block, "ply", pairs)

    return (
        [along_dom(step, block) for step, block in zip(far_steps(count), blocks)]
        + [along_ply(start, block) for start, block in zip((0, 1), blocks[4:])]
        + [along_dom(step, block) for step, block in zip(near_steps(count), blocks[6:])]
    )


def body(state, star, flux, cluster, neighbour, orient, plane, thick,
         stiffness, trace_maps, lift_maps, rotations):
    stars = star.transpose(1, 2, 0, 3).reshape(Q * Q, 3, E).astype(F32)
    flux = flux.transpose(0, 2, 3, 1, 4).reshape(2 * Q * Q, 4, E)
    trace_maps = trace_maps.transpose(1, 0, 2)
    lift_maps = lift_maps.transpose(2, 0, 1)
    marks = jnp.concatenate(
        [
            neighbour,
            orient,
            cluster.reshape(1, E),
            jnp.pad(thick, ((0, 0), (0, E - LAY))),
            jnp.zeros((PLANE - THICK - 2, E), jnp.int32),
            plane.reshape(-1, E),
        ],
        axis=0,
    )
    kept = [shape((3 * PAD, WIDE), BF16), shape((4 * AP, WIDE)), shape((Q, 40, E))]
    sends = [shape(dims) for dims in SENDS]
    split = shape((2 * Q * AP, ALL), BF16)
    products = [shape((3 * rows, 3 * PAD), BF16) for rows, _ in STEPS[:3]]
    own_outs = [kept[2], kept[1], shape((2 * AP, Q * ALL), BF16)]
    x_early, coarse, *steps = call(
        first_kernel, (state, stars, stiffness), [kept[0], kept[2]] + products,
        [PADDED, PADDED, X, Y], 100_000_000,
    )
    s_early, l_early, hot, traces, *out_early = call(
        first_send_kernel, (x_early, trace_maps, marks),
        [kept[1], split, shape((CP, ALL), BF16), shape((4 * AP, 3 * PAD), BF16)] + sends,
        [], 100_000_000,
    )
    in_early = exchange(out_early)
    held, own, near, solvers, same, volumes, lifts, turns = call(
        early_own_kernel,
        (state, x_early, s_early, l_early, stars, flux, marks, stiffness, lift_maps, rotations),
        own_outs + [
            shape((2 * Q * Q, 4, E)), shape((ALL, ALL), BF16), shape((120, 3 * PAD), BF16),
            shape((40, 12 * AP), BF16), shape((3 * AP, 3 * AP), BF16),
        ],
        [pltpu.VMEM((Q, 40, E), F32), Y], 200_000_000,
    )
    middle, x_late, s_late, l_late, *out_late = call(
        middle_kernel,
        (held, own, near, coarse, hot, marks, stars, solvers, lifts, turns, *steps, traces,
         *in_early),
        [kept[2], kept[0], kept[1], split] + sends,
        [PADDED, PADDED, X, Y, SIDE, STACK], 200_000_000,
    )
    in_late = exchange(out_late)
    held, own, near = call(
        late_own_kernel, (middle, x_late, s_late, l_late, stars, solvers, volumes, same),
        own_outs, [Y], 200_000_000,
    )
    return call(
        last_kernel, (held, own, near, hot, marks, solvers, lifts, turns, *in_late),
        shape((Q, B, E)), [SIDE, STACK], 100_000_000,
    )


def solution(mesh):
    both = ("dom", "ply")
    in_specs = (
        P(None, None, both),
        P(None, None, None, both),
        P(None, None, None, None, both),
        P(both),
        P(None, both),
        P(None, both),
        P(both, None),
        P(both, None),
        P(),
        P(),
        P(),
        P(),
    )
    return jax.shard_map(
        body, mesh=mesh, in_specs=in_specs, out_specs=P(None, None, both), check_vma=False
    )
```

```python
import jax
import jax.numpy as jnp
from jax import lax
from jax.experimental import pallas as pl
from jax.experimental.pallas import tpu as pltpu
from jax.sharding import PartitionSpec as P

F32, BF16 = jnp.float32, jnp.bfloat16
Q, B, A, ORDER = 9, 35, 15, 5
E = 128
PAD = 48
AP = 16
THICK, PLANE = 9, 16
SLOT, LAY = 8, 16
CUTS = 5 * SLOT + 2 * LAY
CP = 80
WIDE = Q * E
ALL = 4 * E

EARLY = [0.5 ** (k + 1) for k in range(ORDER)]
LATE = [1.0 - 0.5 ** (k + 1) for k in range(ORDER)]
FACT = [1.0, 2.0, 6.0, 24.0, 120.0]
STEPS = [(24, 48), (16, 48), (8, 32), (8, 16)]


def dot(a, b):
    return jnp.dot(a, b, preferred_element_type=F32)


def halves(x):
    top = x.astype(BF16)
    return top, (x - top.astype(F32)).astype(BF16)


def tripled(a):
    top = a.astype(BF16).astype(F32)
    return jnp.concatenate([top, top, a - top], axis=1).astype(BF16)


def padded(a, rows, cols):
    r, c = a.shape
    if c < cols:
        a = jnp.concatenate([a, jnp.zeros((r, cols - c), a.dtype)], axis=1)
    if r < rows:
        a = jnp.concatenate([a, jnp.zeros((rows - r, cols), a.dtype)], axis=0)
    return a


def lanes(p):
    return slice(p * E, (p + 1) * E)


def put_stack(ref, p, value, at=0, reach=PAD):
    top, rest = halves(value)
    for n, part in enumerate((top, rest, top)):
        ref[n * reach + at : n * reach + at + value.shape[0], lanes(p)] = part


def stiff_rows(stiffness):
    return [tripled(padded(stiffness[d][0:24], 24, PAD)).astype(F32) for d in range(3)]


def trace_rows(trace_maps):
    blocks = [tripled(padded(trace_maps[:, f, :], AP, PAD)).astype(F32) for f in range(4)]
    return jnp.concatenate(blocks, axis=0).astype(BF16)


def volume_rows(stiffness):
    blocks = [tripled(padded(stiffness[d].T, 40, PAD)).astype(F32) for d in range(3)]
    return jnp.concatenate(blocks, axis=0).astype(BF16)


def lift_rows(lift_maps):
    return tripled(jnp.concatenate([padded(lift_maps[:, f, :].T, 40, AP) for f in range(4)], axis=1))


def turn_rows(face_rotations):
    blocks = [tripled(padded(face_rotations[h], AP, AP)).astype(F32) for h in range(3)]
    return jnp.concatenate(blocks, axis=0)


def widen(source, target, blocks):
    for n in range(blocks):
        target[n] = source[n].astype(F32)


def star_apply(y, stars, rows):
    def one(p, total):
        total = list(total)
        at = pl.ds(pl.multiple_of(p * E, E), E)
        for d in range(3):
            value = y[d * rows : (d + 1) * rows, at]
            for q in range(Q):
                total[q] = total[q] + stars[q * Q + p, d : d + 1, :] * value
        return tuple(total)

    start = tuple(jnp.zeros((rows, E), F32) for _ in range(Q))
    return lax.fori_loop(0, Q, one, start, unroll=Q)


def taylor(first, steps, stars, x, y, add):
    values = [first[q] for q in range(Q)]
    for k, (rows, writes) in enumerate(STEPS):
        for p in range(Q):
            put_stack(x, p, padded(values[p], writes, E))
        y[0 : 3 * rows, :] = dot(steps[k][...], x[...])
        values = star_apply(y, stars, rows)
        for q in range(Q):
            add(k + 1, q, rows, values[q])


def far_steps(count):
    return (count - 1, 3, count - 3, count // 2)


def near_steps(count):
    return (1,)


def shared_faces(marks):
    dom, ply = lax.axis_index("dom"), lax.axis_index("ply")
    count = lax.axis_size("dom")
    odd, high = lax.rem(dom, 2), lax.rem(ply, 2)

    def column(row, start):
        dims = (SLOT, row.shape[1])
        sub = lax.broadcasted_iota(jnp.int32, dims, 0)
        lane = lax.broadcasted_iota(jnp.int32, dims, 1)
        picked = jnp.where(lane == sub + start, row.astype(F32), 0.0)
        return jnp.sum(picked, axis=1, keepdims=True)

    def plane_column(step):
        peer = lax.rem(dom + jnp.where(odd == 0, step, count - step), count)
        tile = E // SLOT
        return column(marks[pl.ds(PLANE + peer // tile, 1), :], lax.rem(peer, tile) * SLOT)

    def thick_columns(row):
        values = marks[pl.ds(THICK + row, 1), :]
        return [column(values, half) for half in (0, SLOT)]

    return (
        [plane_column(step) for step in far_steps(count)]
        + thick_columns(1 - high)
        + thick_columns(high)
        + [plane_column(step) for step in near_steps(count)]
    )


def pick_shared(marks, hot):
    columns = shared_faces(marks)
    columns.append(jnp.full((SLOT, 1), -1.0, F32))
    lane = lax.broadcasted_iota(jnp.int32, (AP, E), 1).astype(F32)
    for n in range(0, len(columns), 2):
        column = jnp.concatenate(columns[n : n + 2], axis=0)
        for f in range(4):
            hot[n * SLOT : (n + 2) * SLOT, lanes(f)] = jnp.where(
                column == lane + float(f * E), 1.0, 0.0
            ).astype(BF16)


def send_traces(s, hot, l, outs):
    split_traces(s, l)
    parts = lax.dot_general(
        l[...], hot[...], (((1,), (1,)), ((), ())), preferred_element_type=F32
    )
    total = (parts[0 : Q * AP] + parts[Q * AP : 2 * Q * AP]).T
    at = 0
    for out in outs[:-1]:
        out[...] = total[at : at + out.shape[0]]
        at += out.shape[0]
    outs[-1][...] = jnp.zeros_like(outs[-1])
    outs[-1][0:SLOT] = total[at : at + SLOT]


def split_traces(s, l):
    for q in range(Q):
        for f in range(4):
            top, rest = halves(s[f * AP : (f + 1) * AP, lanes(q)])
            l[q * AP : (q + 1) * AP, lanes(f)] = top
            l[Q * AP + q * AP : Q * AP + (q + 1) * AP, lanes(f)] = rest


def first_kernel(state, stars, stiffness, trace_maps, marks,
                 x_out, s_out, coarse, hot, l, step1, step2, step3, traces, *rest):
    sends, (first, early, x, y) = rest[:7], rest[7:]
    steps = (step1, step2, step3, step3)
    blocks = stiff_rows(stiffness)
    for step, (rows, _) in zip(steps, STEPS):
        step[...] = jnp.concatenate([block[0:rows] for block in blocks], axis=0).astype(BF16)
    traces[...] = trace_rows(trace_maps)
    pick_shared(marks, hot)
    first[...] = jnp.zeros_like(first)
    first[:, 0:B, :] = state[...]
    early[...] = first[...] * EARLY[0]
    coarse[...] = first[:, 0:40, :] * LATE[0]

    def add(k, q, rows, value):
        sign = -1.0 if k % 2 else 1.0
        early[q, 0:rows, :] = early[q, 0:rows, :] + value * (sign * EARLY[k] / FACT[k])
        coarse[q, 0:rows, :] = coarse[q, 0:rows, :] + value * (sign * LATE[k] / FACT[k])

    taylor(first, steps, stars, x, y, add)
    for p in range(Q):
        put_stack(x_out, p, early[p])
    s_out[...] = dot(traces[...], x_out[...])
    send_traces(s_out, hot, l, sends)


def put_near(near, picked):
    for q in range(Q):
        cols = slice(q * ALL, (q + 1) * ALL)
        near[0:AP, cols] = picked[q * AP : (q + 1) * AP].astype(BF16)
        near[AP : 2 * AP, cols] = picked[(Q + q) * AP : (Q + q + 1) * AP].astype(BF16)


def own_part(base, x, s, l, stars, solvers, volumes, same, held, own, near, y):
    put_near(near, dot(l[...], same[...]))
    y[...] = dot(volumes[...], x[...])
    sums = star_apply(y, stars, 40)
    for q in range(Q):
        held[q] = base(q) + sums[q]
    for f, rows, total in fluxes(solvers, 0, s, None):
        for q in range(Q):
            own[rows, lanes(q)] = total[q]


def fluxes(solvers, side, values, before):
    for f in range(4):
        rows = slice(f * AP, (f + 1) * AP)

        def face(p, total):
            total = list(total)
            at = pl.ds(pl.multiple_of(p * E, E), E)
            value = values[rows, at]
            for q in range(Q):
                total[q] = total[q] + solvers[(side * Q + q) * Q + p, f : f + 1, :] * value
            return tuple(total)

        start = [jnp.zeros((AP, E), F32) if before is None else before[rows, lanes(q)] for q in range(Q)]
        total = lax.fori_loop(0, Q, face, tuple(start), unroll=Q)
        yield f, rows, total


def early_own_kernel(state, x, s, l, stars, flux, marks, stiffness, lift_maps, rotations,
                     held, own, near, solvers, same, volumes, lifts, turns, padded_state, y):
    widen(flux, solvers, 2 * Q * Q)
    sub = lax.broadcasted_iota(jnp.int32, (ALL, E), 0)
    for f in range(4):
        same[:, lanes(f)] = jnp.where(sub == marks[f : f + 1, :], 1.0, 0.0).astype(BF16)
    volumes[...] = volume_rows(stiffness)
    lifts[...] = lift_rows(lift_maps)
    turns[...] = turn_rows(rotations).astype(BF16)
    padded_state[...] = jnp.zeros_like(padded_state)
    padded_state[:, 0:B, :] = state[...]
    own_part(lambda q: padded_state[q], x, s, l, stars, solvers, volumes, same, held, own, near, y)


def late_own_kernel(middle, x, s, l, stars, solvers, volumes, same, held, own, near, y):
    own_part(lambda q: middle[q], x, s, l, stars, solvers, volumes, same, held, own, near, y)


def finished(held, own, near, arrived, hot, marks, solvers, lifts, turns, o, g):
    landed = jnp.concatenate(
        [ref[...] for ref in arrived[:-1]]
        + [arrived[-1][0:SLOT], jnp.zeros((CP - CUTS, Q * AP), F32)],
        axis=0,
    )
    pieces = [
        lax.dot_general(piece, hot[...], (((0,), (0,)), ((), ())), preferred_element_type=F32)
        for piece in halves(landed)
    ]
    ways = [jnp.broadcast_to(marks[4 + f : 5 + f, :], (AP, E)) for f in range(4)]
    masks = [(way == 0, way == 1) for way in ways]
    for q in range(Q):
        cols = slice(q * ALL, (q + 1) * ALL)
        top = near[0:AP, cols] + pieces[0][q * AP : (q + 1) * AP].astype(BF16)
        rest = near[AP : 2 * AP, cols] + pieces[1][q * AP : (q + 1) * AP].astype(BF16)
        turned = dot(turns[...], jnp.concatenate([top, rest, top], axis=0))
        for f in range(4):
            first, second = masks[f]
            o[f * AP : (f + 1) * AP, lanes(q)] = jnp.where(
                first,
                turned[0:AP, lanes(f)],
                jnp.where(second, turned[AP : 2 * AP, lanes(f)], turned[2 * AP : 3 * AP, lanes(f)]),
            )
    for f, rows, total in fluxes(solvers, 1, o, own):
        for q in range(Q):
            put_stack(g, q, total[q], f * AP, 4 * AP)
    results = []
    for q in range(0, Q, 2):
        group = range(q, min(q + 2, Q))
        lifted = dot(lifts[...], g[:, q * E : (group[-1] + 1) * E])
        results += [held[n] - lifted[:, lanes(n - q)] for n in group]
    return results


def middle_kernel(held, own, near, coarse, hot, marks, stars, solvers, lifts, turns,
                  step1, step2, step3, traces, *rest):
    arrived, (middle, x_out, s_out, l), sends = rest[:7], rest[7:11], rest[11:18]
    first, late, x, y, o, g = rest[18:]
    values = finished(
        held, own, near, arrived, hot, marks, solvers, lifts, turns, o, g
    )
    for q in range(Q):
        first[q] = padded(values[q], PAD, E)
        middle[q] = values[q]
        late[q] = first[q] * EARLY[0]

    def add(k, q, rows, value):
        sign = -1.0 if k % 2 else 1.0
        late[q, 0:rows, :] = late[q, 0:rows, :] + value * (sign * EARLY[k] / FACT[k])

    taylor(first, (step1, step2, step3, step3), stars, x, y, add)
    fine = marks[8:9, :] == 1
    for q in range(Q):
        late[q, 0:40, :] = jnp.where(fine, late[q, 0:40, :], coarse[q])
        put_stack(x_out, q, late[q])
    s_out[...] = dot(traces[...], x_out[...])
    send_traces(s_out, hot, l, sends)


def last_kernel(held, own, near, hot, marks, solvers, lifts, turns, *rest):
    arrived, out, (o, g) = rest[:7], rest[7], rest[8:]
    values = finished(
        held, own, near, arrived, hot, marks, solvers, lifts, turns, o, g
    )
    for q in range(Q):
        out[q] = values[q][0:B]


def shape(dims, kind=F32):
    return jax.ShapeDtypeStruct(dims, kind)


CORE_ROWS = 24
SENDS = (
    [(SLOT, Q * AP)] * 4 + [(LAY, Q * AP)] * 2 + [(CORE_ROWS, Q * AP)]
)
PADDED = pltpu.VMEM((Q, PAD, E), F32)
X = pltpu.VMEM((3 * PAD, WIDE), BF16)
Y = pltpu.VMEM((120, WIDE), F32)
SIDE = pltpu.VMEM((4 * AP, WIDE), F32)
STACK = pltpu.VMEM((12 * AP, WIDE), BF16)


def call(kernel, operands, outs, scratch, flops):
    vmem = pl.BlockSpec(memory_space=pltpu.VMEM)
    return pl.pallas_call(
        kernel,
        out_shape=outs,
        in_specs=[vmem] * len(operands),
        out_specs=jax.tree.map(lambda _: vmem, outs),
        scratch_shapes=scratch,
        compiler_params=pltpu.CompilerParams(vmem_limit_bytes=40 * 1024 * 1024),
        cost_estimate=pl.CostEstimate(flops=flops, bytes_accessed=2_000_000, transcendentals=0),
    )(*operands)


def exchange(blocks):
    count, layers = lax.axis_size("dom"), lax.axis_size("ply")

    def along_dom(step, block):
        if step % 2 == 0:
            pairs = [(i, (i + step) % count) for i in range(count)]
        else:
            pairs = []
            for even in range(0, count, 2):
                other = (even + step) % count
                pairs += [(even, other), (other, even)]
        return lax.ppermute(block, "dom", pairs)

    def along_ply(start, block):
        pairs = []
        for low in range(start, layers - 1, 2):
            pairs += [(low, low + 1), (low + 1, low)]
        return lax.ppermute(block, "ply", pairs)

    return (
        [along_dom(step, block) for step, block in zip(far_steps(count), blocks)]
        + [along_ply(start, block) for start, block in zip((0, 1), blocks[4:])]
        + [along_dom(step, block) for step, block in zip(near_steps(count), blocks[6:])]
    )


def body(state, star, flux, cluster, neighbour, orient, plane, thick,
         stiffness, trace_maps, lift_maps, rotations):
    stars = star.transpose(1, 2, 0, 3).reshape(Q * Q, 3, E).astype(F32)
    flux = flux.transpose(0, 2, 3, 1, 4).reshape(2 * Q * Q, 4, E)
    trace_maps = trace_maps.transpose(1, 0, 2)
    lift_maps = lift_maps.transpose(2, 0, 1)
    marks = jnp.concatenate(
        [
            neighbour,
            orient,
            cluster.reshape(1, E),
            jnp.pad(thick, ((0, 0), (0, E - LAY))),
            jnp.zeros((PLANE - THICK - 2, E), jnp.int32),
            plane.reshape(-1, E),
        ],
        axis=0,
    )
    kept = [shape((3 * PAD, WIDE), BF16), shape((4 * AP, WIDE)), shape((Q, 40, E))]
    sends = [shape(dims) for dims in SENDS]
    split = shape((2 * Q * AP, ALL), BF16)
    products = [shape((3 * rows, 3 * PAD), BF16) for rows, _ in STEPS[:3]]
    products.append(shape((4 * AP, 3 * PAD), BF16))
    own_outs = [kept[2], kept[1], shape((2 * AP, Q * ALL), BF16)]
    x_early, s_early, coarse, hot, l_early, *rest = call(
        first_kernel,
        (state, stars, stiffness, trace_maps, marks),
        kept + [shape((CP, ALL), BF16), split]
        + products + sends,
        [PADDED, PADDED, X, Y],
        100_000_000,
    )
    steps, out_early = rest[:4], rest[4:]
    in_early = exchange(out_early)
    held, own, near, solvers, same, volumes, lifts, turns = call(
        early_own_kernel,
        (state, x_early, s_early, l_early, stars, flux, marks, stiffness, lift_maps, rotations),
        own_outs + [
            shape((2 * Q * Q, 4, E)), shape((ALL, ALL), BF16), shape((120, 3 * PAD), BF16),
            shape((40, 12 * AP), BF16), shape((3 * AP, 3 * AP), BF16),
        ],
        [pltpu.VMEM((Q, 40, E), F32), Y], 200_000_000,
    )
    middle, x_late, s_late, l_late, *out_late = call(
        middle_kernel,
        (held, own, near, coarse, hot, marks, stars, solvers, lifts, turns, *steps,
         *in_early),
        [kept[2], kept[0], kept[1], split] + sends,
        [PADDED, PADDED, X, Y, SIDE, STACK], 200_000_000,
    )
    in_late = exchange(out_late)
    held, own, near = call(
        late_own_kernel, (middle, x_late, s_late, l_late, stars, solvers, volumes, same),
        own_outs, [Y], 200_000_000,
    )
    return call(
        last_kernel, (held, own, near, hot, marks, solvers, lifts, turns, *in_late),
        shape((Q, B, E)), [SIDE, STACK], 100_000_000,
    )


def solution(mesh):
    both = ("dom", "ply")
    in_specs = (
        P(None, None, both),
        P(None, None, None, both),
        P(None, None, None, None, both),
        P(both),
        P(None, both),
        P(None, both),
        P(both, None),
        P(both, None),
        P(),
        P(),
        P(),
        P(),
    )
    return jax.shard_map(
        body, mesh=mesh, in_specs=in_specs, out_specs=P(None, None, both), check_vma=False
    )
```

```python
import jax
import jax.numpy as jnp
from jax import lax
from jax.experimental import pallas as pl
from jax.experimental.pallas import tpu as pltpu
from jax.sharding import PartitionSpec as P

F32, BF16 = jnp.float32, jnp.bfloat16
Q, B, A, ORDER = 9, 35, 15, 5
E = 128
PAD = 48
AP = 16
THICK, PLANE = 9, 11
SLOT, LAY = 8, 16
CUTS = 5 * SLOT + 2 * LAY
CP = 80
WIDE = Q * E
ALL = 4 * E

EARLY = [0.5 ** (k + 1) for k in range(ORDER)]
LATE = [1.0 - 0.5 ** (k + 1) for k in range(ORDER)]
FACT = [1.0, 2.0, 6.0, 24.0, 120.0]
STEPS = [(24, 48), (16, 48), (8, 32), (8, 16)]


def dot(a, b):
    return jnp.dot(a, b, preferred_element_type=F32)


def halves(x):
    top = x.astype(BF16)
    return top, (x - top.astype(F32)).astype(BF16)


def tripled(a):
    top = a.astype(BF16).astype(F32)
    return jnp.concatenate([top, top, a - top], axis=1).astype(BF16)


def padded(a, rows, cols):
    r, c = a.shape
    if c < cols:
        a = jnp.concatenate([a, jnp.zeros((r, cols - c), a.dtype)], axis=1)
    if r < rows:
        a = jnp.concatenate([a, jnp.zeros((rows - r, cols), a.dtype)], axis=0)
    return a


def lanes(p):
    return slice(p * E, (p + 1) * E)


def put_stack(ref, p, value, at=0, reach=PAD):
    top, rest = halves(value)
    for n, part in enumerate((top, rest, top)):
        ref[n * reach + at : n * reach + at + value.shape[0], lanes(p)] = part


def stiff_rows(stiffness):
    return [tripled(padded(stiffness[d][0:24], 24, PAD)).astype(F32) for d in range(3)]


def trace_rows(trace_maps):
    blocks = [tripled(padded(trace_maps[:, f, :], AP, PAD)).astype(F32) for f in range(4)]
    return jnp.concatenate(blocks, axis=0).astype(BF16)


def volume_rows(stiffness):
    blocks = [tripled(padded(stiffness[d].T, 40, PAD)).astype(F32) for d in range(3)]
    return jnp.concatenate(blocks, axis=0).astype(BF16)


def lift_rows(lift_maps):
    return tripled(jnp.concatenate([padded(lift_maps[:, f, :].T, 40, AP) for f in range(4)], axis=1))


def turn_rows(face_rotations):
    blocks = [tripled(padded(face_rotations[h], AP, AP)).astype(F32) for h in range(3)]
    return jnp.concatenate(blocks, axis=0)


def widen(source, target, blocks):
    for n in range(blocks):
        target[n] = source[n].astype(F32)


def star_apply(y, stars, rows):
    def one(p, total):
        total = list(total)
        at = pl.ds(pl.multiple_of(p * E, E), E)
        for d in range(3):
            value = y[d * rows : (d + 1) * rows, at]
            for q in range(Q):
                total[q] = total[q] + stars[q * Q + p, d : d + 1, :] * value
        return tuple(total)

    start = tuple(jnp.zeros((rows, E), F32) for _ in range(Q))
    return lax.fori_loop(0, Q, one, start, unroll=Q if rows < 40 else 3)


def taylor(first, steps, stars, x, y, add):
    values = [first[q] for q in range(Q)]
    for k, (rows, writes) in enumerate(STEPS):
        for p in range(Q):
            put_stack(x, p, padded(values[p], writes, E))
        y[0 : 3 * rows, :] = dot(steps[k][...], x[...])
        values = star_apply(y, stars, rows)
        for q in range(Q):
            add(k + 1, q, rows, values[q])


def far_steps(count):
    return (count - 1, 3, count - 3, count // 2)


def near_steps(count):
    return (1,)


def shared_faces(marks):
    dom, ply = lax.axis_index("dom"), lax.axis_index("ply")
    count = lax.axis_size("dom")
    odd, high = lax.rem(dom, 2), lax.rem(ply, 2)

    def column(row, start):
        dims = (SLOT, row.shape[1])
        sub = lax.broadcasted_iota(jnp.int32, dims, 0)
        lane = lax.broadcasted_iota(jnp.int32, dims, 1)
        picked = jnp.where(lane == sub + start, row.astype(F32), 0.0)
        return jnp.sum(picked, axis=1, keepdims=True)

    def plane_column(step):
        peer = lax.rem(dom + jnp.where(odd == 0, step, count - step), count)
        tile = E // SLOT
        return column(marks[pl.ds(PLANE + peer // tile, 1), :], lax.rem(peer, tile) * SLOT)

    def thick_columns(row):
        values = marks[pl.ds(THICK + row, 1), :]
        return [column(values, half) for half in (0, SLOT)]

    return (
        [plane_column(step) for step in far_steps(count)]
        + thick_columns(1 - high)
        + thick_columns(high)
        + [plane_column(step) for step in near_steps(count)]
    )


def pick_shared(marks, hot):
    columns = shared_faces(marks)
    columns.append(jnp.full((SLOT, 1), -1.0, F32))
    lane = lax.broadcasted_iota(jnp.int32, (AP, E), 1).astype(F32)
    for n in range(0, len(columns), 2):
        column = jnp.concatenate(columns[n : n + 2], axis=0)
        for f in range(4):
            hot[n * SLOT : (n + 2) * SLOT, lanes(f)] = jnp.where(
                column == lane + float(f * E), 1.0, 0.0
            ).astype(BF16)


def send_traces(s, hot, l, outs):
    split_traces(s, l)
    total = None
    for part in (1, 0):
        piece = lax.dot_general(
            hot[...],
            l[part * Q * AP : (part + 1) * Q * AP, :],
            (((1,), (1,)), ((), ())),
            preferred_element_type=F32,
        )
        total = piece if total is None else total + piece
    at = 0
    for out in outs[:-1]:
        out[...] = total[at : at + out.shape[0]]
        at += out.shape[0]
    outs[-1][...] = jnp.zeros_like(outs[-1])
    outs[-1][0:SLOT] = total[at : at + SLOT]


def split_traces(s, l):
    for q in range(Q):
        for f in range(4):
            top, rest = halves(s[f * AP : (f + 1) * AP, lanes(q)])
            l[q * AP : (q + 1) * AP, lanes(f)] = top
            l[Q * AP + q * AP : Q * AP + (q + 1) * AP, lanes(f)] = rest


def first_kernel(state, stars, stiffness, trace_maps, marks,
                 x_out, s_out, coarse, hot, l, step1, step2, step3, traces, *rest):
    sends, (first, early, x, y) = rest[:7], rest[7:]
    steps = (step1, step2, step3, step3)
    blocks = stiff_rows(stiffness)
    for step, (rows, _) in zip(steps, STEPS):
        step[...] = jnp.concatenate([block[0:rows] for block in blocks], axis=0).astype(BF16)
    traces[...] = trace_rows(trace_maps)
    pick_shared(marks, hot)
    first[...] = jnp.zeros_like(first)
    first[:, 0:B, :] = state[...]
    early[...] = first[...] * EARLY[0]
    coarse[...] = first[:, 0:40, :] * LATE[0]

    def add(k, q, rows, value):
        sign = -1.0 if k % 2 else 1.0
        early[q, 0:rows, :] = early[q, 0:rows, :] + value * (sign * EARLY[k] / FACT[k])
        coarse[q, 0:rows, :] = coarse[q, 0:rows, :] + value * (sign * LATE[k] / FACT[k])

    taylor(first, steps, stars, x, y, add)
    for p in range(Q):
        put_stack(x_out, p, early[p])
    s_out[...] = dot(traces[...], x_out[...])
    send_traces(s_out, hot, l, sends)


def put_near(near, picked):
    for q in range(Q):
        cols = slice(q * ALL, (q + 1) * ALL)
        near[0:AP, cols] = picked[q * AP : (q + 1) * AP].astype(BF16)
        near[AP : 2 * AP, cols] = picked[(Q + q) * AP : (Q + q + 1) * AP].astype(BF16)


def own_part(base, x, s, l, stars, solvers, volumes, same, held, own, near, y):
    put_near(near, dot(l[...], same[...]))
    y[...] = dot(volumes[...], x[...])
    sums = star_apply(y, stars, 40)
    for q in range(Q):
        held[q] = base(q) + sums[q]
    for f, rows, total in fluxes(solvers, 0, s, None):
        for q in range(Q):
            own[rows, lanes(q)] = total[q]


def fluxes(solvers, side, values, before):
    for f in range(4):
        rows = slice(f * AP, (f + 1) * AP)

        def face(p, total):
            total = list(total)
            at = pl.ds(pl.multiple_of(p * E, E), E)
            value = values[rows, at]
            for q in range(Q):
                total[q] = total[q] + solvers[(side * Q + q) * Q + p, f : f + 1, :] * value
            return tuple(total)

        start = [jnp.zeros((AP, E), F32) if before is None else before[rows, lanes(q)] for q in range(Q)]
        total = lax.fori_loop(0, Q, face, tuple(start), unroll=Q)
        yield f, rows, total


def early_own_kernel(state, x, s, l, stars, flux, marks, stiffness, lift_maps, rotations,
                     held, own, near, solvers, same, volumes, lifts, turns, padded_state, y):
    widen(flux, solvers, 2 * Q * Q)
    sub = lax.broadcasted_iota(jnp.int32, (ALL, E), 0)
    for f in range(4):
        same[:, lanes(f)] = jnp.where(sub == marks[f : f + 1, :], 1.0, 0.0).astype(BF16)
    volumes[...] = volume_rows(stiffness)
    lifts[...] = lift_rows(lift_maps)
    turns[...] = turn_rows(rotations).astype(BF16)
    padded_state[...] = jnp.zeros_like(padded_state)
    padded_state[:, 0:B, :] = state[...]
    own_part(lambda q: padded_state[q], x, s, l, stars, solvers, volumes, same, held, own, near, y)


def late_own_kernel(middle, x, s, l, stars, solvers, volumes, same, held, own, near, y):
    own_part(lambda q: middle[q], x, s, l, stars, solvers, volumes, same, held, own, near, y)


def finished(held, own, near, arrived, hot, marks, solvers, lifts, turns, o, g):
    landed = jnp.concatenate(
        [ref[...] for ref in arrived[:-1]]
        + [arrived[-1][0:SLOT], jnp.zeros((CP - CUTS, Q * AP), F32)],
        axis=0,
    )
    pieces = [
        lax.dot_general(piece, hot[...], (((0,), (0,)), ((), ())), preferred_element_type=F32)
        for piece in halves(landed)
    ]
    ways = [jnp.broadcast_to(marks[4 + f : 5 + f, :], (AP, E)) for f in range(4)]
    masks = [(way == 0, way == 1) for way in ways]
    for q in range(Q):
        cols = slice(q * ALL, (q + 1) * ALL)
        top = near[0:AP, cols] + pieces[0][q * AP : (q + 1) * AP].astype(BF16)
        rest = near[AP : 2 * AP, cols] + pieces[1][q * AP : (q + 1) * AP].astype(BF16)
        turned = dot(turns[...], jnp.concatenate([top, rest, top], axis=0))
        for f in range(4):
            first, second = masks[f]
            o[f * AP : (f + 1) * AP, lanes(q)] = jnp.where(
                first,
                turned[0:AP, lanes(f)],
                jnp.where(second, turned[AP : 2 * AP, lanes(f)], turned[2 * AP : 3 * AP, lanes(f)]),
            )
    for f, rows, total in fluxes(solvers, 1, o, own):
        for q in range(Q):
            put_stack(g, q, total[q], f * AP, 4 * AP)
    results = []
    for q in range(0, Q, 2):
        group = range(q, min(q + 2, Q))
        lifted = dot(lifts[...], g[:, q * E : (group[-1] + 1) * E])
        results += [held[n] - lifted[:, lanes(n - q)] for n in group]
    return results


def middle_kernel(held, own, near, coarse, hot, marks, stars, solvers, lifts, turns,
                  step1, step2, step3, traces, *rest):
    arrived, (middle, x_out, s_out, l), sends = rest[:7], rest[7:11], rest[11:18]
    first, late, x, y, o, g = rest[18:]
    values = finished(
        held, own, near, arrived, hot, marks, solvers, lifts, turns, o, g
    )
    for q in range(Q):
        first[q] = padded(values[q], PAD, E)
        middle[q] = values[q]
        late[q] = first[q] * EARLY[0]

    def add(k, q, rows, value):
        sign = -1.0 if k % 2 else 1.0
        late[q, 0:rows, :] = late[q, 0:rows, :] + value * (sign * EARLY[k] / FACT[k])

    taylor(first, (step1, step2, step3, step3), stars, x, y, add)
    fine = marks[8:9, :] == 1
    for q in range(Q):
        late[q, 0:40, :] = jnp.where(fine, late[q, 0:40, :], coarse[q])
        put_stack(x_out, q, late[q])
    s_out[...] = dot(traces[...], x_out[...])
    send_traces(s_out, hot, l, sends)


def last_kernel(held, own, near, hot, marks, solvers, lifts, turns, *rest):
    arrived, out, (o, g) = rest[:7], rest[7], rest[8:]
    values = finished(
        held, own, near, arrived, hot, marks, solvers, lifts, turns, o, g
    )
    for q in range(Q):
        out[q] = values[q][0:B]


def shape(dims, kind=F32):
    return jax.ShapeDtypeStruct(dims, kind)


CORE_ROWS = 24
SENDS = (
    [(SLOT, Q * AP)] * 4 + [(LAY, Q * AP)] * 2 + [(CORE_ROWS, Q * AP)]
)
PADDED = pltpu.VMEM((Q, PAD, E), F32)
X = pltpu.VMEM((3 * PAD, WIDE), BF16)
Y = pltpu.VMEM((120, WIDE), F32)
SIDE = pltpu.VMEM((4 * AP, WIDE), F32)
STACK = pltpu.VMEM((12 * AP, WIDE), BF16)


def call(kernel, operands, outs, scratch, flops):
    vmem = pl.BlockSpec(memory_space=pltpu.VMEM)
    return pl.pallas_call(
        kernel,
        out_shape=outs,
        in_specs=[vmem] * len(operands),
        out_specs=jax.tree.map(lambda _: vmem, outs),
        scratch_shapes=scratch,
        compiler_params=pltpu.CompilerParams(vmem_limit_bytes=40 * 1024 * 1024),
        cost_estimate=pl.CostEstimate(flops=flops, bytes_accessed=2_000_000, transcendentals=0),
    )(*operands)


def exchange(blocks):
    count, layers = lax.axis_size("dom"), lax.axis_size("ply")

    def along_dom(step, block):
        if step % 2 == 0:
            pairs = [(i, (i + step) % count) for i in range(count)]
        else:
            pairs = []
            for even in range(0, count, 2):
                other = (even + step) % count
                pairs += [(even, other), (other, even)]
        return lax.ppermute(block, "dom", pairs)

    def along_ply(start, block):
        pairs = []
        for low in range(start, layers - 1, 2):
            pairs += [(low, low + 1), (low + 1, low)]
        return lax.ppermute(block, "ply", pairs)

    return (
        [along_dom(step, block) for step, block in zip(far_steps(count), blocks)]
        + [along_ply(start, block) for start, block in zip((0, 1), blocks[4:])]
        + [along_dom(step, block) for step, block in zip(near_steps(count), blocks[6:])]
    )


def body(state, star, flux, cluster, neighbour, orient, plane, thick,
         stiffness, trace_maps, lift_maps, rotations):
    stars = star.transpose(1, 2, 0, 3).reshape(Q * Q, 3, E).astype(F32)
    flux = flux.transpose(0, 2, 3, 1, 4).reshape(2 * Q * Q, 4, E)
    trace_maps = trace_maps.transpose(1, 0, 2)
    lift_maps = lift_maps.transpose(2, 0, 1)
    marks = jnp.concatenate(
        [
            neighbour,
            orient,
            cluster.reshape(1, E),
            jnp.pad(thick, ((0, 0), (0, E - LAY))),
            plane.reshape(-1, E),
        ],
        axis=0,
    )
    kept = [shape((3 * PAD, WIDE), BF16), shape((4 * AP, WIDE)), shape((Q, 40, E))]
    sends = [shape(dims) for dims in SENDS]
    split = shape((2 * Q * AP, ALL), BF16)
    products = [shape((3 * rows, 3 * PAD), BF16) for rows, _ in STEPS[:3]]
    products.append(shape((4 * AP, 3 * PAD), BF16))
    own_outs = [kept[2], kept[1], shape((2 * AP, Q * ALL), BF16)]
    x_early, s_early, coarse, hot, l_early, *rest = call(
        first_kernel,
        (state, stars, stiffness, trace_maps, marks),
        kept + [shape((CP, ALL), BF16), split]
        + products + sends,
        [PADDED, PADDED, X, Y],
        100_000_000,
    )
    steps, out_early = rest[:4], rest[4:]
    in_early = exchange(out_early)
    held, own, near, solvers, same, volumes, lifts, turns = call(
        early_own_kernel,
        (state, x_early, s_early, l_early, stars, flux, marks, stiffness, lift_maps, rotations),
        own_outs + [
            shape((2 * Q * Q, 4, E)), shape((ALL, ALL), BF16), shape((120, 3 * PAD), BF16),
            shape((40, 12 * AP), BF16), shape((3 * AP, 3 * AP), BF16),
        ],
        [pltpu.VMEM((Q, 40, E), F32), Y], 200_000_000,
    )
    middle, x_late, s_late, l_late, *out_late = call(
        middle_kernel,
        (held, own, near, coarse, hot, marks, stars, solvers, lifts, turns, *steps,
         *in_early),
        [kept[2], kept[0], kept[1], split] + sends,
        [PADDED, PADDED, X, Y, SIDE, STACK], 200_000_000,
    )
    in_late = exchange(out_late)
    held, own, near = call(
        late_own_kernel, (middle, x_late, s_late, l_late, stars, solvers, volumes, same),
        own_outs, [Y], 200_000_000,
    )
    return call(
        last_kernel, (held, own, near, hot, marks, solvers, lifts, turns, *in_late),
        shape((Q, B, E)), [SIDE, STACK], 100_000_000,
    )


def solution(mesh):
    both = ("dom", "ply")
    in_specs = (
        P(None, None, both),
        P(None, None, None, both),
        P(None, None, None, None, both),
        P(both),
        P(None, both),
        P(None, both),
        P(both, None),
        P(both, None),
        P(),
        P(),
        P(),
        P(),
    )
    return jax.shard_map(
        body, mesh=mesh, in_specs=in_specs, out_specs=P(None, None, both), check_vma=False
    )
```
